512 devices in a mesh: dp: 128 (over x, y_lo, z), pair: 4 (over y_hi, core).
Axes of the slice: x: 4, y: 8 (y_hi: 2, y_lo: 4; y = y_hi * 4 + y_lo), z: 8, core: 2. Of those that a mesh axis runs over, the one named last changes fastest.
Arguments:
- image_emb: bfloat16 [65536, 1152], P(('dp', 'pair')), may hold values from -0.19921875 to 0.19921875
- text_emb: bfloat16 [65536, 1152], P(('dp', 'pair')), may hold values from -0.19921875 to 0.19921875
- head_weight: bfloat16 [1152, 1152], replicated, may hold values from -0.1875 to 0.1875
- natural_exponent_multiplier: float32 [1], replicated, may hold values from 1.5 to 2.5
- bias: float32 [1], replicated, may hold values from -7 to -4
Outputs:
- loss: float32 [65536], P(('dp', 'pair'))
- image_grad: float32 [65536, 1152], P(('dp', 'pair'))
- text_grad: float32 [65536, 1152], P(('dp', 'pair'))
- head_grad: float32 [1152, 1152], P('dp', 'pair')
The draws below stay inside these ranges and needn't reach their ends.
All inputs are finite; a program needn't handle non-finite values.
Results may differ from the reference program's by a relative error of at most 0.0051.
Values may be sent and summed in bfloat16 or wider, within the bound.
A program may use at most 64 MiB of HBM per device.

```python
import jax
import jax.numpy as jnp
from jax import lax

D = 1152
WINDOW = 3
GROUP = 512
B_TOTAL = 65536
N_DP = 128


def levels(rng, shape, split, low, high):
    gain = 1.0
    for dim, parts in split:
        steps = jax.random.uniform(jax.random.fold_in(jax.random.fold_in(rng, 6), dim), (parts,), jnp.float32, low / len(split), high / len(split))
        gain = gain * jnp.repeat(jnp.exp(steps), shape[dim] // parts).reshape((-1,) + (1,) * (len(shape) - 1 - dim))
    return gain


def normal_values(rng, shape, scale, most, split=(), kind=jnp.bfloat16):
    result = scale * jax.random.normal(rng, shape, jnp.float32)
    if split:
        result = result * levels(rng, shape, split, -0.22, 0.18)
    return jnp.clip(result, -most, most).astype(kind)


def setup_inputs(seed: int = 0) -> dict:
    keys = jax.random.split(jax.random.key(seed), 6)
    image_emb = normal_values(keys[0], (B_TOTAL, D), 0.03, 0.19921875, ((0, 512),))
    text_emb = normal_values(keys[1], (B_TOTAL, D), 0.03, 0.19921875, ((0, 512),))
    head_weight = normal_values(keys[2], (D, D), D ** -0.5, 0.1875)
    natural_exponent_multiplier = jnp.clip(jax.random.uniform(keys[3], (1,), jnp.float32, 1.5, 2.5), 1.5, 2.5)
    bias = jnp.clip(jax.random.uniform(keys[4], (1,), jnp.float32, -7.0, -4.0), -7.0, -4.0)
    return dict(image_emb=image_emb, text_emb=text_emb, head_weight=head_weight, natural_exponent_multiplier=natural_exponent_multiplier, bias=bias)


epsilon = 1e-06

def reference(image_emb, text_emb, head_weight, natural_exponent_multiplier, bias):
    similarity_sharpness_factor = jnp.exp(natural_exponent_multiplier[0])
    similarity_additive_shift = bias[0]
    projected = jnp.dot(image_emb, head_weight, preferred_element_type=jnp.float32)
    image_scale = lax.rsqrt(lax.optimization_barrier(jnp.sum(projected * projected, axis=1, keepdims=True)) + epsilon)
    image_unit = projected * image_scale
    picture_embedding_matrix = image_unit.astype(jnp.bfloat16)
    text_wide = text_emb.astype(jnp.float32)
    text_scale = lax.rsqrt(lax.optimization_barrier(jnp.sum(text_wide * text_wide, axis=1, keepdims=True)) + epsilon)
    text_unit = text_wide * text_scale
    text_feat = text_unit.astype(jnp.bfloat16)
    picture_piece_sequence = picture_embedding_matrix.astype(jnp.float32).reshape(N_DP, GROUP, D)
    text_blocks = text_feat.astype(jnp.float32).reshape(N_DP, GROUP, D)
    diagonal = jnp.eye(GROUP, dtype=jnp.float32)
    loss_rows = jnp.zeros((N_DP, GROUP), jnp.float32)
    image_dir = jnp.zeros((N_DP, GROUP, D), jnp.float32)
    text_dir = jnp.zeros((N_DP, GROUP, D), jnp.float32)
    for rotation_shift_amount in range(WINDOW):
        arriving_picture_piece = jnp.roll(text_blocks, rotation_shift_amount, axis=0)
        similarity_matrix_entries = similarity_sharpness_factor * jnp.einsum('xcz,xvz->xcv', picture_piece_sequence, arriving_picture_piece) + similarity_additive_shift
        matching_target_sign = diagonal * (1.0 if rotation_shift_amount == 0 else 0.0)
        loss_rows = loss_rows + lax.optimization_barrier(jnp.sum(jax.nn.softplus(similarity_matrix_entries) - matching_target_sign * similarity_matrix_entries, axis=2))
        reduced_precision_weighting = (similarity_sharpness_factor * (jax.nn.sigmoid(similarity_matrix_entries) - matching_target_sign)).astype(jnp.bfloat16)
        objective_weighting_factor = lax.optimization_barrier(reduced_precision_weighting).astype(jnp.float32)
        image_dir = image_dir + jnp.einsum('agh,ahc->agc', objective_weighting_factor, arriving_picture_piece)
        text_part = jnp.einsum('agh,agc->ahc', objective_weighting_factor, picture_piece_sequence)
        text_dir = text_dir + jnp.roll(text_part, -rotation_shift_amount, axis=0)
    image_dir = image_dir.reshape(B_TOTAL, D)
    text_dir = text_dir.reshape(B_TOTAL, D)
    along = lax.optimization_barrier(jnp.sum(image_unit * image_dir, axis=1, keepdims=True))
    pre_grad = (image_scale * (image_dir - image_unit * along)).astype(jnp.bfloat16)
    image_grad = jnp.dot(pre_grad, head_weight.T, preferred_element_type=jnp.float32)
    head_grad = jnp.dot(image_emb.T, pre_grad, preferred_element_type=jnp.float32)
    text_along = lax.optimization_barrier(jnp.sum(text_unit * text_dir, axis=1, keepdims=True))
    text_grad = text_scale * (text_dir - text_unit * text_along)
    loss = loss_rows.reshape(B_TOTAL)
    return (loss, image_grad, text_grad, head_grad)
```

```python
import functools

import jax
import jax.numpy as jnp
import numpy as np
from jax import lax
from jax.experimental import pallas as pl
from jax.experimental.pallas import tpu as pltpu
from jax.sharding import PartitionSpec as P

NX, NYL, NZ = 4, 4, 8
NY = 2 * NYL
WINDOW = 3
ROWS = 128
BLOCK = 2 * ROWS
D = 1152
COLS = D // 4
PIECE = 80
HALF = 8 * PIECE
EPS = 1e-06
BF = jnp.bfloat16
F32 = jnp.float32

R_RAW, R_SIB, R_LOSS, R_EMB, R_PRE, R_ONE, R_FIN, R_ALL = 12, 13, 14, 15, 18, 21, 35, 43
S_K, S_RAW, S_Q, S_SIB, S_LOSS, S_EMB, S_PRE, S_ONE, S_FIN, S_ALL = 0, 10, 11, 12, 13, 14, 17, 20, 34, 50


def nt(left, right):
    return lax.dot_general(left, right, (((1,), (1,)), ((), ())), preferred_element_type=F32)


def nn(left, right):
    return jnp.dot(left, right, preferred_element_type=F32)


def select_matrix():
    row = np.arange(2 * HALF)
    half, piece, k = row // HALF, (row % HALF) // PIECE, row % PIECE
    block, inner = k // 9, k % 9
    source = np.where(half == 0, 72 * piece + k, 576 + 72 * block + 9 * piece + inner)
    return ((source[:, None] == np.arange(D)[None, :]) & (k < 72)[:, None]).astype(np.float32)


def kernel(
    nem, bias, img, txt, w_any, sel_any,
    loss_o, ig_o, tg_o, hg_o,
    w, sel, kbuf, raw, qf, unit, acc, pre, pre_t, sib_f32, sib_bf, loss_s, loss_r,
    emb_t, p_t, p_out, one, fin_s, fin_r, ssem, rsem, lsem,
):
    dp = lax.axis_index("dp")
    pair = lax.axis_index("pair")
    core = lax.rem(pair, 2)
    yh = lax.div(pair, 2)
    x = lax.div(dp, NYL * NZ)
    yl = lax.rem(lax.div(dp, NZ), NYL)
    z = lax.rem(dp, NZ)
    y = yh * NYL + yl

    def chip(cx, cy, cz, cc):
        return (cx * (NYL * NZ) + lax.rem(cy, NYL) * NZ + cz, lax.div(cy, NYL) * 2 + cc)

    sibling = (dp, yh * 2 + 1 - core)
    across = (dp, (1 - yh) * 2 + core)
    flip_to = jnp.where(lax.rem(dp, 32) == 31 * (1 - core), 1, 0)
    flip_from = jnp.where(lax.rem(dp, 32) == 31 * core, 1, 0)
    chain_to = (lax.rem(dp + 1 + 126 * core, 128), lax.rem(yh + flip_to, 2) * 2 + core)
    chain_from = (lax.rem(dp + 127 - 126 * core, 128), lax.rem(yh + flip_from, 2) * 2 + core)

    def x_dev(d):
        return chip(lax.rem(x + d, NX), y, z, core)

    def one_dev(h, d):
        if h == 0:
            return chip(x, lax.rem(y + d, NY), z, core)
        return chip(x, y, lax.rem(z + d, NZ), core)

    def fin_block(h, d):
        return lax.rem(z + d, 8) if h == 0 else lax.rem(y + d, 8)

    def fin_dev(h, d):
        block = fin_block(h, d)
        return (8 * y + block if h == 0 else 64 + 8 * block + z, x)

    low = jnp.where(dp < 64, 1, 0)
    q8 = lax.rem(lax.div(dp, 8), 8)

    def fin_from(d):
        ys = jnp.where(low == 1, q8, lax.rem(q8 + 8 - d, 8))
        zs = jnp.where(low == 1, lax.rem(z + 8 - d, 8), z)
        return chip(pair, ys, zs, 0)

    def is_me(device):
        return jnp.logical_and(device[0] == dp, device[1] == pair)

    barrier = pltpu.get_barrier_semaphore()

    def hello(device):
        pl.semaphore_signal(barrier, inc=1, device_id=device, device_id_type=pl.DeviceIdType.MESH)

    def copy(src, dst, send, recv, device):
        return pltpu.make_async_remote_copy(
            src_ref=src, dst_ref=dst, send_sem=ssem.at[send], recv_sem=rsem.at[recv],
            device_id=device, device_id_type=pl.DeviceIdType.MESH,
        )

    def normal(value):
        scale = lax.rsqrt(jnp.sum(value * value, axis=1, keepdims=True) + EPS)
        return value * scale, scale

    def run(role):
        own, oth = role, 1 - role
        own_rows = pl.ds(own * ROWS, ROWS)
        oth_rows = pl.ds(oth * ROWS, ROWS)
        w_copy = pltpu.make_async_copy(w_any, w, lsem.at[0])
        w_copy.start()
        hello(sibling)
        hello(across)
        hello(chain_from)
        if role == 0:
            sel_copy = pltpu.make_async_copy(sel_any, sel, lsem.at[1])
            sel_copy.start()
            for d in range(1, NX):
                hello(x_dev(NX - d))
            for h in range(2):
                for d in range(1, 8):
                    hello(one_dev(h, 8 - d))
        for d in range(8):
            device = fin_from(d)
            pl.when(jnp.logical_not(is_me(device)))(lambda device=device: hello(device))

        started = []

        def go(*args):
            c = copy(*args)
            c.start()
            started.append(c)

        def kslot(t, h, s):
            return kbuf.at[t, h, pl.ds(s * ROWS, ROWS)]

        def arrived(dst, recv):
            copy(dst, dst, 0, recv, sibling).wait_recv()

        def spread(s, send):
            go(kslot(0, 0, s), kslot(1, 0, s), send, 4 + s, chain_to)
            go(kslot(0, 0, s), kslot(0, 1, s), send + 1, 2 + s, across)

        t_unit, t_scale = normal(txt[...].astype(F32))
        if role == 0:
            kbuf[0, 0, own_rows] = t_unit.astype(BF)
            away = 3 + 3 + 14 + 16
            for h in range(2):
                for d in range(8):
                    away = away - jnp.where(is_me(fin_dev(h, d)), 1, 0)
            pl.semaphore_wait(barrier, away)
            spread(own, S_K)
            go(txt, raw.at[own_rows], S_RAW, R_RAW, sibling)
            w_copy.wait()
            i_unit, i_scale = normal(nn(img[...], w[...]))
            unit[own_rows] = i_unit
            qf[own_rows] = i_unit.astype(BF)
            go(qf.at[own_rows], kslot(0, 0, own), S_Q, own, sibling)
            raw[own_rows] = img[...]
        else:
            unit[own_rows] = t_unit
            qf[own_rows] = t_unit.astype(BF)
            pl.semaphore_wait(barrier, 3)
            go(qf.at[own_rows], kslot(0, 0, own), S_Q, own, sibling)
            go(img, raw.at[own_rows], S_RAW, R_RAW, sibling)
            w_copy.wait()
            i_unit, i_scale = normal(nn(img[...], w[...]))
            kbuf[0, 0, own_rows] = i_unit.astype(BF)
            spread(own, S_K)
            raw[own_rows] = txt[...]
        own_scale = i_scale if role == 0 else t_scale
        arrived(kslot(0, 0, oth), oth)
        spread(oth, S_K + 2)
        arrived(raw.at[oth_rows], R_RAW)
        if role == 0:
            o_unit, oth_scale = normal(nn(raw[oth_rows], w[...]))
        else:
            o_unit, oth_scale = normal(raw[oth_rows].astype(F32))
        unit[oth_rows] = o_unit
        qf[oth_rows] = o_unit.astype(BF)

        gain = jnp.exp(jnp.full((1, 1), nem[0], F32))
        shift = bias[0]
        if role == 0:
            sel_copy.wait()
            for part in range(4):
                rows = pl.ds(part * (HALF // 2), HALF // 2)
                emb_t[0, rows] = nt(sel[rows], raw[...]).astype(BF)
            for d in range(1, NX):
                go(emb_t.at[0], emb_t.at[d], S_EMB + d - 1, R_EMB + d - 1, x_dev(d))

        loss = jnp.zeros((BLOCK, 1), F32)

        def score(t, h, loss):
            k = kbuf[t, h]
            s = gain * nt(qf[...], k) + shift
            e = jnp.exp(-jnp.abs(s))
            sig = jnp.where(s >= 0, 1.0, e) / (1.0 + e)
            label = None
            if t == 0 and h == 0:
                r = lax.broadcasted_iota(jnp.int32, (BLOCK, BLOCK), 0)
                c = lax.broadcasted_iota(jnp.int32, (BLOCK, BLOCK), 1)
                label = jnp.where(r == c, 1.0, 0.0)
                sig = sig - label
            if role == 0:
                term = jnp.maximum(s, 0.0) + jnp.log1p(e)
                if label is not None:
                    term = term - label * s
                loss = loss + jnp.sum(term, axis=1, keepdims=True)
            value = nn((gain * sig).astype(BF), k)
            if label is not None:
                acc[...] = value
            else:
                acc[...] += value
            return loss

        loss = score(0, 0, loss)
        send = S_K + 4
        for t, h in ((1, 0), (0, 1), (1, 1)):
            for s in (own, oth):
                arrived(kslot(t, h, s), 4 * t + 2 * h + s)
                go(kslot(t, h, s), kslot(t + 1, h, s), send, 4 * t + 4 + 2 * h + s, chain_to)
                send += 1
            loss = score(t, h, loss)
        for h in range(2):
            for s in (own, oth):
                arrived(kslot(2, h, s), 8 + 2 * h + s)
            loss = score(2, h, loss)

        for half_rows, scale in ((own_rows, own_scale), (oth_rows, oth_scale)):
            u = unit[half_rows]
            a = acc[half_rows]
            along = jnp.sum(u * a, axis=1, keepdims=True)
            g = scale * (a - u * along)
            if role == 0:
                pre[half_rows] = g.astype(BF)
                pre_t[:, half_rows] = jnp.transpose(g).astype(BF)
            elif half_rows is own_rows:
                tg_o[...] = g
            else:
                unit[half_rows] = g

        if role == 0:
            for d in range(1, NX):
                start = pl.multiple_of(lax.rem(x + d, NX) * COLS, 16)
                go(pre_t.at[pl.ds(start, COLS)], p_t.at[d], S_PRE + d - 1, R_PRE + d - 1, x_dev(d))
            go(pre.at[oth_rows], sib_bf, S_SIB, R_SIB, sibling)
            turned = jnp.transpose(jnp.broadcast_to(loss, (BLOCK, 128)))
            loss_o[...] = turned[0:1, 0:ROWS]
            loss_s[...] = turned[0:8, ROWS:BLOCK]
            go(loss_s, loss_r, S_LOSS, R_LOSS, sibling)
            start = pl.multiple_of(x * COLS, 16)
            p_t[0] = pre_t[pl.ds(start, COLS)]
            for d in range(1, NX):
                arrived(p_t.at[d], R_PRE + d - 1)
                arrived(emb_t.at[d], R_EMB + d - 1)

            def product(h, d):
                index = lax.rem((y if h == 0 else z) + d, 8)
                rows = pl.ds(pl.multiple_of(h * HALF + index * PIECE, 16), PIECE)
                total = nt(emb_t[0, rows], p_t[0])
                for k in range(1, NX):
                    total = total + nt(emb_t[k, rows], p_t[k])
                return total

            for d in (4, 3, 5, 2, 6, 1, 7):
                for h in range(2):
                    i = 7 * h + d - 1
                    p_out[i] = product(h, d).astype(BF)
                    go(p_out.at[i], one.at[i], S_ONE + i, R_ONE + i, one_dev(h, d))
            totals = [product(0, 0), product(1, 0)]
            ig_o[...] = nt(pre[own_rows], w[...])
            r = lax.broadcasted_iota(jnp.int32, (128, PIECE), 0)
            c = lax.broadcasted_iota(jnp.int32, (128, PIECE), 1)
            inner = jnp.bitwise_and(r, 15)
            pick = jnp.logical_and(inner < 9, c == 9 * jnp.right_shift(r, 4) + inner)
            pick = jnp.where(pick, 1.0, 0.0).astype(BF)
            for h in range(2):
                total = totals[h]
                for d in range(1, 8):
                    i = 7 * h + d - 1
                    arrived(one.at[i], R_ONE + i)
                    total = total + one[i].astype(F32)
                blocks = nn(pick, total.astype(BF)).astype(BF)
                for i in range(8):
                    fin_s[h, i] = blocks[16 * i : 16 * i + 16]
                for d in range(8):
                    device = fin_dev(h, d)
                    block = fin_block(h, d)
                    me = is_me(device)
                    c = copy(fin_s.at[h, block], fin_r.at[d], S_FIN + 8 * h + d, R_FIN + d, device)

                    @pl.when(me)
                    def _(d=d, block=block, h=h):
                        fin_r[d] = fin_s[h, block]

                    @pl.when(jnp.logical_not(me))
                    def _(c=c):
                        c.start()

            arrived(sib_f32, R_SIB)
            tg_o[...] = sib_f32[...]
        else:
            go(unit.at[oth_rows], sib_f32, S_SIB, R_SIB, sibling)
            arrived(sib_bf, R_SIB)
            ig_o[...] = nt(sib_bf[...], w[...])
            arrived(loss_r, R_LOSS)
            loss_o[...] = loss_r[0:1]

        for d in range(8):
            me = is_me(fin_from(d))

            @pl.when(jnp.logical_not(me))
            def _(d=d):
                arrived(fin_r.at[d], R_FIN + d)

        total = fin_r[0].astype(F32)
        for d in range(1, 8):
            total = total + fin_r[d].astype(F32)
        hg_o[...] = total[0:9]
        for c in started:
            c.wait_send()
        if role == 0:
            for h in range(2):
                for d in range(8):
                    device = fin_dev(h, d)
                    c = copy(
                        fin_s.at[h, fin_block(h, d)], fin_r.at[d], S_FIN + 8 * h + d, R_FIN + d, device
                    )
                    pl.when(jnp.logical_not(is_me(device)))(lambda c=c: c.wait_send())

    pl.when(core == 0)(lambda: run(0))
    pl.when(core == 1)(lambda: run(1))


def body(image_emb, text_emb, head_weight, natural_exponent_multiplier, bias):
    vmem = pl.BlockSpec(memory_space=pltpu.VMEM)
    smem = pl.BlockSpec(memory_space=pltpu.SMEM)
    hbm = pl.BlockSpec(memory_space=pl.ANY)
    loss, image_grad, text_grad, head_grad = pl.pallas_call(
        kernel,
        name="contrast",
        out_shape=(
            jax.ShapeDtypeStruct((1, ROWS), F32),
            jax.ShapeDtypeStruct((ROWS, D), F32),
            jax.ShapeDtypeStruct((ROWS, D), F32),
            jax.ShapeDtypeStruct((9, COLS), F32),
        ),
        in_specs=[smem, smem, vmem, vmem, hbm, hbm],
        out_specs=(vmem, vmem, vmem, vmem),
        scratch_shapes=[
            pltpu.VMEM((D, D), BF),
            pltpu.VMEM((2 * HALF, D), BF),
            pltpu.VMEM((WINDOW, 2, BLOCK, D), BF),
            pltpu.VMEM((BLOCK, D), BF),
            pltpu.VMEM((BLOCK, D), BF),
            pltpu.VMEM((BLOCK, D), F32),
            pltpu.VMEM((BLOCK, D), F32),
            pltpu.VMEM((BLOCK, D), BF),
            pltpu.VMEM((D, BLOCK), BF),
            pltpu.VMEM((ROWS, D), F32),
            pltpu.VMEM((ROWS, D), BF),
            pltpu.VMEM((8, ROWS), F32),
            pltpu.VMEM((8, ROWS), F32),
            pltpu.VMEM((NX, 2 * HALF, BLOCK), BF),
            pltpu.VMEM((NX, COLS, BLOCK), BF),
            pltpu.VMEM((14, PIECE, COLS), BF),
            pltpu.VMEM((14, PIECE, COLS), BF),
            pltpu.VMEM((2, 8, 16, COLS), BF),
            pltpu.VMEM((8, 16, COLS), BF),
            pltpu.SemaphoreType.DMA((S_ALL,)),
            pltpu.SemaphoreType.DMA((R_ALL,)),
            pltpu.SemaphoreType.DMA((2,)),
        ],
        compiler_params=pltpu.CompilerParams(
            collective_id=0, has_side_effects=True, vmem_limit_bytes=56 * 2**20
        ),
    )(
        natural_exponent_multiplier,
        bias,
        image_emb,
        text_emb,
        head_weight,
        jnp.asarray(select_matrix(), BF),
    )
    return loss.reshape(ROWS), image_grad, text_grad, head_grad


def solution(mesh):
    return jax.shard_map(
        body,
        mesh=mesh,
        in_specs=(P(("dp", "pair"), None), P(("dp", "pair"), None), P(), P(), P()),
        out_specs=(
            P(("dp", "pair")),
            P(("dp", "pair"), None),
            P(("dp", "pair"), None),
            P("dp", "pair"),
        ),
        check_vma=False,
    )
```

```python
import jax
import jax.numpy as jnp
import numpy as np
from jax import lax
from jax.experimental import pallas as pl
from jax.experimental.pallas import tpu as pltpu
from jax.sharding import PartitionSpec as P

NX, NYL, NZ = 4, 4, 8
NY = 2 * NYL
WINDOW = 3
ROWS = 128
BLOCK = 2 * ROWS
D = 1152
COLS = D // 4
PIECE = 80
PART = 64
PARTS = ROWS // PART
HALF = 8 * PIECE
EPS = 1e-06
BF = jnp.bfloat16
F32 = jnp.float32

R_K, R_TEXT, R_RT, R_RI, R_RAW, R_SIB, R_LOSS, R_EMB, R_PRE = 0, 24, 36, 40, 48, 49, 50, 51, 54
R_ONE, R_FIN, R_ALL = 57, 71, 79
S_RAW, S_SIB, S_LOSS, S_EMB, S_PRE, S_ONE, S_FIN, S_RT, S_RI, S_K, S_ALL = 0, 1, 2, 3, 6, 9, 23, 39, 43, 51, 100


def nt(left, right):
    return lax.dot_general(left, right, (((1,), (1,)), ((), ())), preferred_element_type=F32)


def nn(left, right):
    return jnp.dot(left, right, preferred_element_type=F32)


def select_matrix():
    row = np.arange(2 * HALF)
    half, piece, k = row // HALF, (row % HALF) // PIECE, row % PIECE
    block, inner = k // 9, k % 9
    source = np.where(half == 0, 72 * piece + k, 576 + 72 * block + 9 * piece + inner)
    return ((source[:, None] == np.arange(D)[None, :]) & (k < 72)[:, None]).astype(np.float32)


def kernel(
    nem, bias, img, txt, w_any, sel_any,
    loss_o, ig_o, tg_o, hg_o,
    w, sel, kbuf, tbuf, rt, ri, raw, qf, unit, acc, pre, pre_t, sib_f32, sib_bf, loss_s, loss_r,
    emb_t, p_t, p_out, one, fin_s, fin_r, ssem, rsem, lsem,
):
    dp = lax.axis_index("dp")
    pair = lax.axis_index("pair")
    core = lax.rem(pair, 2)
    yh = lax.div(pair, 2)
    x = lax.div(dp, NYL * NZ)
    yl = lax.rem(lax.div(dp, NZ), NYL)
    z = lax.rem(dp, NZ)
    y = yh * NYL + yl

    def chip(cx, cy, cz, cc):
        return (cx * (NYL * NZ) + lax.rem(cy, NYL) * NZ + cz, lax.div(cy, NYL) * 2 + cc)

    sibling = (dp, yh * 2 + 1 - core)
    across = (dp, (1 - yh) * 2 + core)
    flip_to = jnp.where(lax.rem(dp, 32) == 31 * (1 - core), 1, 0)
    flip_from = jnp.where(lax.rem(dp, 32) == 31 * core, 1, 0)
    chain_to = (lax.rem(dp + 1 + 126 * core, 128), lax.rem(yh + flip_to, 2) * 2 + core)
    chain_from = (lax.rem(dp + 127 - 126 * core, 128), lax.rem(yh + flip_from, 2) * 2 + core)

    column = (lax.rem(dp + jnp.where(z == 0, 7, 121), 128), pair)
    row_up = (lax.rem(dp + 8, 128), lax.rem(yh + jnp.where(yl == 3, 1, 0), 2) * 2 + core)
    row_down = (lax.rem(dp + 120, 128), lax.rem(yh + jnp.where(yl == 0, 1, 0), 2) * 2 + core)

    def x_dev(d):
        return chip(lax.rem(x + d, NX), y, z, core)

    def one_dev(h, d):
        if h == 0:
            return chip(x, lax.rem(y + d, NY), z, core)
        return chip(x, y, lax.rem(z + d, NZ), core)

    def fin_block(h, d):
        return lax.rem(z + d, 8) if h == 0 else lax.rem(y + d, 8)

    def fin_dev(h, d):
        block = fin_block(h, d)
        return (8 * y + block if h == 0 else 64 + 8 * block + z, x)

    low = jnp.where(dp < 64, 1, 0)
    q8 = lax.rem(lax.div(dp, 8), 8)

    def fin_from(d):
        ys = jnp.where(low == 1, q8, lax.rem(q8 + 8 - d, 8))
        zs = jnp.where(low == 1, lax.rem(z + 8 - d, 8), z)
        return chip(pair, ys, zs, 0)

    def is_me(device):
        return jnp.logical_and(device[0] == dp, device[1] == pair)

    barrier = pltpu.get_barrier_semaphore()

    def hello(device):
        pl.semaphore_signal(barrier, inc=1, device_id=device, device_id_type=pl.DeviceIdType.MESH)

    def copy(src, dst, send, recv, device):
        return pltpu.make_async_remote_copy(
            src_ref=src, dst_ref=dst, send_sem=ssem.at[send], recv_sem=rsem.at[recv],
            device_id=device, device_id_type=pl.DeviceIdType.MESH,
        )

    def normal(value):
        scale = lax.rsqrt(jnp.sum(value * value, axis=1, keepdims=True) + EPS)
        return value * scale, scale

    def run(role):
        own, oth = role, 1 - role
        own_rows = pl.ds(own * ROWS, ROWS)
        oth_rows = pl.ds(oth * ROWS, ROWS)
        w_copy = pltpu.make_async_copy(w_any, w, lsem.at[0])
        w_copy.start()
        hello(sibling)
        hello(across)
        hello(chain_from)
        hello(chain_to)

        @pl.when(z == 0)
        def _():
            hello(column)
            hello(row_down)

        if role == 1:

            @pl.when(z == NZ - 1)
            def _():
                hello(column)
                hello(row_up)

        at_wrap = jnp.where(jnp.logical_or(z == 0, z == NZ - 1), 1 + role, 0)
        if role == 0:
            sel_copy = pltpu.make_async_copy(sel_any, sel, lsem.at[1])
            sel_copy.start()
            for d in range(1, NX):
                hello(x_dev(NX - d))
            for h in range(2):
                for d in range(1, 8):
                    hello(one_dev(h, 8 - d))
        for d in range(8):
            device = fin_from(d)
            pl.when(jnp.logical_not(is_me(device)))(lambda device=device: hello(device))

        started = []
        next_send = [S_K]

        def go(*args):
            c = copy(*args)
            c.start()
            started.append(c)

        def move(src, dst, recv, device):
            go(src, dst, next_send[0], recv, device)
            next_send[0] += 1

        def kslot(t, h, s, u):
            return kbuf.at[t, h, pl.ds(s * ROWS + u * PART, PART)]

        def k_sem(t, h, s, u):
            return R_K + 8 * t + 4 * h + 2 * s + u

        def arrived(dst, recv):
            copy(dst, dst, 0, recv, sibling).wait_recv()

        text_to = chain_to if role == 0 else chain_from

        def tslot(t, h, u):
            return kslot(t, h, 0, u) if role == 0 else tbuf.at[t, h, pl.ds(u * PART, PART)]

        def t_sem(t, h, u):
            return R_TEXT + 4 * t + 2 * h + u

        def chain(src, dst, recv, device, h, wrap, relay_dst, relay_recv):
            if h == 1:
                move(src, dst, recv, device)
                return
            direct = copy(src, dst, next_send[0], recv, device)
            relayed = copy(src, relay_dst, next_send[0], relay_recv, column)
            next_send[0] += 1
            pl.when(z != wrap)(lambda: direct.start())
            pl.when(z == wrap)(lambda: relayed.start())
            started.append(direct)

        def text_on(t, h, parts=range(PARTS)):
            for u in parts:
                if t or h:
                    arrived(tslot(t, h, u), t_sem(t, h, u))
                if t < WINDOW - 1:
                    chain(
                        tslot(t, h, u), tslot(t + 1, h, u), t_sem(t + 1, h, u), text_to, h,
                        NZ - 1, rt.at[min(t, 1), pl.ds(u * PART, PART)], R_RT + 2 * t + u,
                    )
                if t == 0 and h == 0:
                    move(tslot(0, 0, u), tslot(0, 1, u), t_sem(0, 1, u), across)
                if role == 1:
                    move(tslot(t, h, u), kslot(t, h, 1, u), k_sem(t, h, 1, u), sibling)

        def image_on(t, h, parts=((1, 0), (1, 1), (0, 0), (0, 1))):
            for s, u in parts:
                if t or h or s == 0:
                    arrived(kslot(t, h, s, u), k_sem(t, h, s, u))
                if t < WINDOW - 1:
                    chain(
                        kslot(t, h, s, u), kslot(t + 1, h, s, u), k_sem(t + 1, h, s, u), chain_to, h,
                        0, ri.at[min(t, 1), pl.ds(s * ROWS + u * PART, PART)],
                        R_RI + 4 * t + 2 * s + u,
                    )

        later = []

        def relay(src, dst, recv_in, send, recv_out, device, where):
            c = copy(src, dst, send, recv_out, device)

            @pl.when(z == where)
            def _():
                arrived(src, recv_in)
                c.start()

            later.append((c, where))

        def relay_text(t):
            for u in range(PARTS):
                relay(
                    rt.at[t, pl.ds(u * PART, PART)], tslot(t + 1, 0, u), R_RT + 2 * t + u,
                    S_RT + 2 * t + u, t_sem(t + 1, 0, u), row_up, 0,
                )

        def relay_image(t):
            for s, u in ((1, 0), (1, 1), (0, 0), (0, 1)):
                i = 4 * t + 2 * s + u
                relay(
                    ri.at[t, pl.ds(s * ROWS + u * PART, PART)], kslot(t + 1, 0, s, u), R_RI + i,
                    S_RI + i, k_sem(t + 1, 0, s, u), row_down, NZ - 1,
                )

        t_unit, t_scale = normal(txt[...].astype(F32))
        w_copy.wait()
        i_unit, i_scale = normal(nn(img[...], w[...]))
        if role == 0:
            kbuf[0, 0, own_rows] = t_unit.astype(BF)
            unit[own_rows] = i_unit
            qf[own_rows] = i_unit.astype(BF)
            raw[own_rows] = img[...]
            away = 4 + 3 + 14 + 16 + at_wrap
            for h in range(2):
                for d in range(8):
                    away = away - jnp.where(is_me(fin_dev(h, d)), 1, 0)
            pl.semaphore_wait(barrier, away)
            text_on(0, 0)
            for u in range(PARTS):
                move(qf.at[pl.ds(u * PART, PART)], kslot(0, 0, 0, u), k_sem(0, 0, 0, u), sibling)
            go(txt, raw.at[own_rows], S_RAW, R_RAW, sibling)
            arrived(raw.at[oth_rows], R_RAW)
            o_unit, oth_scale = normal(nn(raw[oth_rows], w[...]))
        else:
            tbuf[0, 0] = t_unit.astype(BF)
            unit[own_rows] = t_unit
            qf[own_rows] = t_unit.astype(BF)
            kbuf[0, 0, own_rows] = i_unit.astype(BF)
            raw[own_rows] = txt[...]
            pl.semaphore_wait(barrier, 4 + at_wrap)
            text_on(0, 0)
            go(img, raw.at[own_rows], S_RAW, R_RAW, sibling)
            image_on(0, 0)
            arrived(raw.at[oth_rows], R_RAW)
            o_unit, oth_scale = normal(raw[oth_rows].astype(F32))
        own_scale = i_scale if role == 0 else t_scale
        unit[oth_rows] = o_unit
        qf[oth_rows] = o_unit.astype(BF)

        gain = jnp.exp(jnp.full((1, 1), nem[0], F32))
        shift = bias[0]

        loss = jnp.zeros((BLOCK, 1), F32)

        def score(t, h, loss):
            k = kbuf[t, h]
            s = gain * nt(qf[...], k) + shift
            e = jnp.exp(-jnp.abs(s))
            sig = jnp.where(s >= 0, 1.0, e) / (1.0 + e)
            label = None
            if t == 0 and h == 0:
                r = lax.broadcasted_iota(jnp.int32, (BLOCK, BLOCK), 0)
                c = lax.broadcasted_iota(jnp.int32, (BLOCK, BLOCK), 1)
                label = jnp.where(r == c, 1.0, 0.0)
                sig = sig - label
            if role == 0:
                term = jnp.maximum(s, 0.0) + jnp.log1p(e)
                if label is not None:
                    term = term - label * s
                loss = loss + jnp.sum(term, axis=1, keepdims=True)
            value = nn((gain * sig).astype(BF), k)
            if label is not None:
                acc[...] = value
            else:
                acc[...] += value
            return loss

        if role == 0:

            def ready(t, h):
                for u in range(PARTS):
                    arrived(kslot(t, h, 1, u), k_sem(t, h, 1, u))

            ready(0, 0)
            loss = score(0, 0, loss)
            sel_copy.wait()
            for part in range(4):
                rows = pl.ds(part * (HALF // 2), HALF // 2)
                emb_t[0, rows] = nt(sel[rows], raw[...]).astype(BF)
            for d in range(1, NX):
                go(emb_t.at[0], emb_t.at[d], S_EMB + d - 1, R_EMB + d - 1, x_dev(d))
            relay_text(0)
            text_on(1, 0)
            text_on(0, 1)
            relay_text(1)
            ready(1, 0)
            loss = score(1, 0, loss)
            text_on(1, 1)
            ready(0, 1)
            loss = score(0, 1, loss)
            text_on(2, 0)
            ready(2, 0)
            loss = score(2, 0, loss)
            ready(1, 1)
            loss = score(1, 1, loss)
            text_on(2, 1)
            ready(2, 1)
            loss = score(2, 1, loss)
        else:
            relay_text(0)
            relay_image(0)
            text_on(1, 0)
            image_on(1, 0)
            text_on(0, 1, (0,))
            for s in (1, 0):
                for u in range(PARTS):
                    move(kslot(0, 0, s, u), kslot(0, 1, s, u), k_sem(0, 1, s, u), across)
            text_on(0, 1, (1,))
            relay_text(1)
            text_on(1, 1)
            text_on(2, 0)
            relay_image(1)
            loss = score(0, 0, loss)
            text_on(2, 1)
            loss = score(1, 0, loss)
            order = ((1, 0), (1, 1), (0, 0), (0, 1))
            image_on(0, 1, order[:2])
            for i in range(2):
                image_on(1, 1, order[i : i + 1])
                image_on(0, 1, order[i + 2 : i + 3])
            loss = score(0, 1, loss)
            image_on(1, 1, order[2:])
            loss = score(1, 1, loss)
            for h in range(2):
                image_on(2, h)
                loss = score(2, h, loss)

        for half_rows, scale in ((own_rows, own_scale), (oth_rows, oth_scale)):
            u = unit[half_rows]
            a = acc[half_rows]
            along = jnp.sum(u * a, axis=1, keepdims=True)
            g = scale * (a - u * along)
            if role == 0:
                pre[half_rows] = g.astype(BF)
                pre_t[:, half_rows] = jnp.transpose(g).astype(BF)
            elif half_rows is own_rows:
                tg_o[...] = g
            else:
                unit[half_rows] = g

        if role == 0:
            for d in range(1, NX):
                start = pl.multiple_of(lax.rem(x + d, NX) * COLS, 16)
                go(pre_t.at[pl.ds(start, COLS)], p_t.at[d], S_PRE + d - 1, R_PRE + d - 1, x_dev(d))
            go(pre.at[oth_rows], sib_bf, S_SIB, R_SIB, sibling)
            turned = jnp.transpose(jnp.broadcast_to(loss, (BLOCK, 128)))
            loss_o[...] = turned[0:1, 0:ROWS]
            loss_s[...] = turned[0:8, ROWS:BLOCK]
            go(loss_s, loss_r, S_LOSS, R_LOSS, sibling)
            start = pl.multiple_of(x * COLS, 16)
            p_t[0] = pre_t[pl.ds(start, COLS)]
            for d in range(1, NX):
                arrived(p_t.at[d], R_PRE + d - 1)
                arrived(emb_t.at[d], R_EMB + d - 1)

            def product(h, d):
                index = lax.rem((y if h == 0 else z) + d, 8)
                rows = pl.ds(pl.multiple_of(h * HALF + index * PIECE, 16), PIECE)
                total = nt(emb_t[0, rows], p_t[0])
                for k in range(1, NX):
                    total = total + nt(emb_t[k, rows], p_t[k])
                return total

            for d in (4, 3, 5, 2, 6, 1, 7):
                for h in range(2):
                    i = 7 * h + d - 1
                    p_out[i] = product(h, d).astype(BF)
                    go(p_out.at[i], one.at[i], S_ONE + i, R_ONE + i, one_dev(h, d))
            totals = [product(0, 0), product(1, 0)]
            ig_o[...] = nt(pre[own_rows], w[...])
            r = lax.broadcasted_iota(jnp.int32, (128, PIECE), 0)
            c = lax.broadcasted_iota(jnp.int32, (128, PIECE), 1)
            inner = jnp.bitwise_and(r, 15)
            pick = jnp.logical_and(inner < 9, c == 9 * jnp.right_shift(r, 4) + inner)
            pick = jnp.where(pick, 1.0, 0.0).astype(BF)
            for h in range(2):
                total = totals[h]
                for d in range(1, 8):
                    i = 7 * h + d - 1
                    arrived(one.at[i], R_ONE + i)
                    total = total + one[i].astype(F32)
                blocks = nn(pick, total.astype(BF)).astype(BF)
                for i in range(8):
                    fin_s[h, i] = blocks[16 * i : 16 * i + 16]
                for d in range(8):
                    device = fin_dev(h, d)
                    block = fin_block(h, d)
                    me = is_me(device)
                    c = copy(fin_s.at[h, block], fin_r.at[d], S_FIN + 8 * h + d, R_FIN + d, device)

                    @pl.when(me)
                    def _(d=d, block=block, h=h):
                        fin_r[d] = fin_s[h, block]

                    @pl.when(jnp.logical_not(me))
                    def _(c=c):
                        c.start()

            arrived(sib_f32, R_SIB)
            tg_o[...] = sib_f32[...]
        else:
            go(unit.at[oth_rows], sib_f32, S_SIB, R_SIB, sibling)
            arrived(sib_bf, R_SIB)
            ig_o[...] = nt(sib_bf[...], w[...])
            arrived(loss_r, R_LOSS)
            loss_o[...] = loss_r[0:1]

        for d in range(8):
            me = is_me(fin_from(d))

            @pl.when(jnp.logical_not(me))
            def _(d=d):
                arrived(fin_r.at[d], R_FIN + d)

        total = fin_r[0].astype(F32)
        for d in range(1, 8):
            total = total + fin_r[d].astype(F32)
        hg_o[...] = total[0:9]
        for c in started:
            c.wait_send()
        for c, where in later:
            pl.when(z == where)(lambda c=c: c.wait_send())
        if role == 0:
            for h in range(2):
                for d in range(8):
                    device = fin_dev(h, d)
                    c = copy(
                        fin_s.at[h, fin_block(h, d)], fin_r.at[d], S_FIN + 8 * h + d, R_FIN + d, device
                    )
                    pl.when(jnp.logical_not(is_me(device)))(lambda c=c: c.wait_send())

    pl.when(core == 0)(lambda: run(0))
    pl.when(core == 1)(lambda: run(1))


def results(loss, ig, tg, hg, loss_o, ig_o, tg_o, hg_o):
    loss_o[...] = loss[0, :]
    ig_o[...] = ig[...]
    tg_o[...] = tg[...]
    hg_o[...] = hg[...]


def body(image_emb, text_emb, head_weight, natural_exponent_multiplier, bias):
    vmem = pl.BlockSpec(memory_space=pltpu.VMEM)
    smem = pl.BlockSpec(memory_space=pltpu.SMEM)
    hbm = pl.BlockSpec(memory_space=pl.ANY)
    loss, image_grad, text_grad, head_grad = pl.pallas_call(
        kernel,
        name="contrast",
        out_shape=(
            jax.ShapeDtypeStruct((1, ROWS), F32),
            jax.ShapeDtypeStruct((ROWS, D), F32),
            jax.ShapeDtypeStruct((ROWS, D), F32),
            jax.ShapeDtypeStruct((9, COLS), F32),
        ),
        in_specs=[smem, smem, vmem, vmem, hbm, hbm],
        out_specs=(vmem, vmem, vmem, vmem),
        scratch_shapes=[
            pltpu.VMEM((D, D), BF),
            pltpu.VMEM((2 * HALF, D), BF),
            pltpu.VMEM((WINDOW, 2, BLOCK, D), BF),
            pltpu.VMEM((WINDOW, 2, ROWS, D), BF),
            pltpu.VMEM((2, ROWS, D), BF),
            pltpu.VMEM((2, BLOCK, D), BF),
            pltpu.VMEM((BLOCK, D), BF),
            pltpu.VMEM((BLOCK, D), BF),
            pltpu.VMEM((BLOCK, D), F32),
            pltpu.VMEM((BLOCK, D), F32),
            pltpu.VMEM((BLOCK, D), BF),
            pltpu.VMEM((D, BLOCK), BF),
            pltpu.VMEM((ROWS, D), F32),
            pltpu.VMEM((ROWS, D), BF),
            pltpu.VMEM((8, ROWS), F32),
            pltpu.VMEM((8, ROWS), F32),
            pltpu.VMEM((NX, 2 * HALF, BLOCK), BF),
            pltpu.VMEM((NX, COLS, BLOCK), BF),
            pltpu.VMEM((14, PIECE, COLS), BF),
            pltpu.VMEM((14, PIECE, COLS), BF),
            pltpu.VMEM((2, 8, 16, COLS), BF),
            pltpu.VMEM((8, 16, COLS), BF),
            pltpu.SemaphoreType.DMA((S_ALL,)),
            pltpu.SemaphoreType.DMA((R_ALL,)),
            pltpu.SemaphoreType.DMA((2,)),
        ],
        compiler_params=pltpu.CompilerParams(
            collective_id=0, has_side_effects=True, vmem_limit_bytes=56 * 2**20
        ),
    )(
        natural_exponent_multiplier,
        bias,
        image_emb,
        text_emb,
        head_weight,
        jnp.asarray(select_matrix(), BF),
    )
    return tuple(
        pl.pallas_call(
            results,
            name="results",
            out_shape=(
                jax.ShapeDtypeStruct((ROWS,), F32),
                jax.ShapeDtypeStruct((ROWS, D), F32),
                jax.ShapeDtypeStruct((ROWS, D), F32),
                jax.ShapeDtypeStruct((9, COLS), F32),
            ),
            in_specs=[vmem] * 4,
            out_specs=(vmem,) * 4,
        )(loss, image_grad, text_grad, head_grad)
    )


def solution(mesh):
    return jax.shard_map(
        body,
        mesh=mesh,
        in_specs=(P(("dp", "pair"), None), P(("dp", "pair"), None), P(), P(), P()),
        out_specs=(
            P(("dp", "pair")),
            P(("dp", "pair"), None),
            P(("dp", "pair"), None),
            P("dp", "pair"),
        ),
        check_vma=False,
    )
```

```python
import jax
import jax.numpy as jnp
import numpy as np
from jax import lax
from jax.experimental import pallas as pl
from jax.experimental.pallas import tpu as pltpu
from jax.sharding import PartitionSpec as P

NX, NYL, NZ = 4, 4, 8
NY = 2 * NYL
WINDOW = 3
ROWS = 128
BLOCK = 2 * ROWS
D = 1152
COLS = D // 4
PIECE = 80
PART = 64
PARTS = ROWS // PART
BOTH = tuple((s, u) for s in (1, 0) for u in range(PARTS))
HALF = 8 * PIECE
EPS = 1e-06
BF = jnp.bfloat16
F32 = jnp.float32

R_RAW, R_SIB, R_LOSS, R_EMB, R_PRE, R_ONE, R_FIN, R_K = 0, 1, 2, 3, 6, 12, 26, 34
R_TEXT = R_K + 12 * PARTS
R_RT = R_TEXT + 6 * PARTS
R_RI = R_RT + 2 * PARTS
R_ALL = R_RI + 4 * PARTS
S_RAW, S_SIB, S_LOSS, S_EMB, S_PRE, S_ONE, S_FIN, S_RT = 0, 1, 2, 3, 6, 12, 26, 42
S_RI = S_RT + 2 * PARTS
S_K = S_RI + 4 * PARTS
S_ALL = S_K + 24 * PARTS


def nt(left, right):
    return lax.dot_general(left, right, (((1,), (1,)), ((), ())), preferred_element_type=F32)


def nn(left, right):
    return jnp.dot(left, right, preferred_element_type=F32)


def select_matrix():
    row = np.arange(2 * HALF)
    half, piece, k = row // HALF, (row % HALF) // PIECE, row % PIECE
    block, inner = k // 9, k % 9
    source = np.where(half == 0, 72 * piece + k, 576 + 72 * block + 9 * piece + inner)
    return ((source[:, None] == np.arange(D)[None, :]) & (k < 72)[:, None]).astype(np.float32)


def kernel(
    nem, bias, img, txt, w_any, sel_any,
    loss_o, ig_o, tg_o, hg_o,
    w, sel, kbuf, tbuf, rt, ri, raw, qf, unit, acc, pre, pre_t, sib_f32, sib_bf, loss_s, loss_r,
    emb_t, p_t, p_out, p_f32, one, fin_s, fin_r, ssem, rsem, lsem,
):
    dp = lax.axis_index("dp")
    pair = lax.axis_index("pair")
    core = lax.rem(pair, 2)
    yh = lax.div(pair, 2)
    x = lax.div(dp, NYL * NZ)
    yl = lax.rem(lax.div(dp, NZ), NYL)
    z = lax.rem(dp, NZ)
    y = yh * NYL + yl

    def chip(cx, cy, cz, cc):
        return (cx * (NYL * NZ) + lax.rem(cy, NYL) * NZ + cz, lax.div(cy, NYL) * 2 + cc)

    sibling = (dp, yh * 2 + 1 - core)
    across = (dp, (1 - yh) * 2 + core)
    flip_to = jnp.where(lax.rem(dp, 32) == 31 * (1 - core), 1, 0)
    flip_from = jnp.where(lax.rem(dp, 32) == 31 * core, 1, 0)
    chain_to = (lax.rem(dp + 1 + 126 * core, 128), lax.rem(yh + flip_to, 2) * 2 + core)
    chain_from = (lax.rem(dp + 127 - 126 * core, 128), lax.rem(yh + flip_from, 2) * 2 + core)

    column = (lax.rem(dp + jnp.where(z == 0, 7, 121), 128), pair)
    row_up = (lax.rem(dp + 8, 128), lax.rem(yh + jnp.where(yl == 3, 1, 0), 2) * 2 + core)
    row_down = (lax.rem(dp + 120, 128), lax.rem(yh + jnp.where(yl == 0, 1, 0), 2) * 2 + core)

    def x_dev(d):
        return chip(lax.rem(x + d, NX), y, z, core)

    def one_dev(h, d):
        if h == 0:
            return chip(x, lax.rem(y + d, NY), z, core)
        return chip(x, y, lax.rem(z + d, NZ), core)

    def fin_block(h, d):
        return lax.rem(z + d, 8) if h == 0 else lax.rem(y + d, 8)

    def fin_dev(h, d):
        block = fin_block(h, d)
        return (8 * y + block if h == 0 else 64 + 8 * block + z, x)

    low = jnp.where(dp < 64, 1, 0)
    q8 = lax.rem(lax.div(dp, 8), 8)

    def fin_from(d):
        ys = jnp.where(low == 1, q8, lax.rem(q8 + 8 - d, 8))
        zs = jnp.where(low == 1, lax.rem(z + 8 - d, 8), z)
        return chip(pair, ys, zs, 0)

    def is_me(device):
        return jnp.logical_and(device[0] == dp, device[1] == pair)

    barrier = pltpu.get_barrier_semaphore()

    def hello(device):
        pl.semaphore_signal(barrier, inc=1, device_id=device, device_id_type=pl.DeviceIdType.MESH)

    def copy(src, dst, send, recv, device):
        return pltpu.make_async_remote_copy(
            src_ref=src, dst_ref=dst, send_sem=ssem.at[send], recv_sem=rsem.at[recv],
            device_id=device, device_id_type=pl.DeviceIdType.MESH,
        )

    def normal(value):
        scale = lax.rsqrt(jnp.sum(value * value, axis=1, keepdims=True) + EPS)
        return value * scale, scale

    def run(role):
        own, oth = role, 1 - role
        own_rows = pl.ds(own * ROWS, ROWS)
        oth_rows = pl.ds(oth * ROWS, ROWS)
        w_copy = pltpu.make_async_copy(w_any, w, lsem.at[0])
        w_copy.start()
        hello(sibling)
        hello(across)
        hello(chain_from)
        hello(chain_to)

        @pl.when(z == 0)
        def _():
            hello(column)
            hello(row_down)

        if role == 1:

            @pl.when(z == NZ - 1)
            def _():
                hello(column)
                hello(row_up)

        if role == 0:
            hello((chain_from[0], chain_from[1] + 1))
            pl.when(z == 0)(lambda: hello((row_down[0], row_down[1] + 1)))

        at_wrap = jnp.where(jnp.logical_or(z == 0, z == NZ - 1), 1 + role, 0)
        if role == 0:
            sel_copy = pltpu.make_async_copy(sel_any, sel, lsem.at[1])
            sel_copy.start()
            for d in range(1, NX):
                hello(x_dev(NX - d))
            for h in range(2):
                for d in range(1, 8):
                    hello(one_dev(h, 8 - d))
        for d in range(8):
            device = fin_from(d)
            pl.when(jnp.logical_not(is_me(device)))(lambda device=device: hello(device))

        started = []
        next_send = [S_K]

        def go(*args):
            c = copy(*args)
            c.start()
            started.append(c)

        def move(src, dst, recv, device):
            go(src, dst, next_send[0], recv, device)
            next_send[0] += 1

        def kslot(t, h, s, u):
            return kbuf.at[t, h, pl.ds(s * ROWS + u * PART, PART)]

        def k_sem(t, h, s, u):
            return R_K + (4 * t + 2 * h + s) * PARTS + u

        def arrived(dst, recv):
            copy(dst, dst, 0, recv, sibling).wait_recv()

        text_to = chain_to if role == 0 else chain_from

        def tslot(t, h, u):
            return kslot(t, h, 0, u) if role == 0 else tbuf.at[t, h, pl.ds(u * PART, PART)]

        def t_sem(t, h, u):
            return R_TEXT + (2 * t + h) * PARTS + u

        def text_next(t, h, u):
            if role == 1 and t == 1:
                return kslot(2, h, 1, u), k_sem(2, h, 1, u), (text_to[0], text_to[1] - 1)
            return tslot(t + 1, h, u), t_sem(t + 1, h, u), text_to

        def chain(src, dst, recv, device, h, wrap, relay_dst, relay_recv):
            if h == 1:
                move(src, dst, recv, device)
                return
            direct = copy(src, dst, next_send[0], recv, device)
            relayed = copy(src, relay_dst, next_send[0], relay_recv, column)
            next_send[0] += 1
            pl.when(z != wrap)(lambda: direct.start())
            pl.when(z == wrap)(lambda: relayed.start())
            started.append(direct)

        def text_on(t, h, parts=range(PARTS)):
            for u in parts:
                if t or h:
                    arrived(tslot(t, h, u), t_sem(t, h, u))
                if t < WINDOW - 1:
                    dst, recv, device = text_next(t, h, u)
                    chain(
                        tslot(t, h, u), dst, recv, device, h,
                        NZ - 1, rt.at[t, pl.ds(u * PART, PART)], R_RT + PARTS * t + u,
                    )
                if t == 0 and h == 0:
                    move(tslot(0, 0, u), tslot(0, 1, u), t_sem(0, 1, u), across)
                if role == 1:
                    move(tslot(t, h, u), kslot(t, h, 1, u), k_sem(t, h, 1, u), sibling)

        def image_on(t, h, parts=BOTH):
            for s, u in parts:
                if t or h or s == 0:
                    arrived(kslot(t, h, s, u), k_sem(t, h, s, u))
                if t < WINDOW - 1:
                    chain(
                        kslot(t, h, s, u), kslot(t + 1, h, s, u), k_sem(t + 1, h, s, u), chain_to, h,
                        0, ri.at[min(t, 1), pl.ds(s * ROWS + u * PART, PART)],
                        R_RI + (2 * t + s) * PARTS + u,
                    )

        later = []

        def relay(src, dst, recv_in, send, recv_out, device, where):
            c = copy(src, dst, send, recv_out, device)

            @pl.when(z == where)
            def _():
                arrived(src, recv_in)
                c.start()

            later.append((c, where))

        def relay_text(t):
            for u in range(PARTS):
                dst, recv, device = text_next(t, 0, u)
                device = (row_up[0], row_up[1] - 1) if device is not text_to else row_up
                relay(
                    rt.at[t, pl.ds(u * PART, PART)], dst, R_RT + PARTS * t + u,
                    S_RT + PARTS * t + u, recv, device, 0,
                )

        def relay_image(t):
            for s, u in BOTH:
                i = (2 * t + s) * PARTS + u
                relay(
                    ri.at[t, pl.ds(s * ROWS + u * PART, PART)], kslot(t + 1, 0, s, u), R_RI + i,
                    S_RI + i, k_sem(t + 1, 0, s, u), row_down, NZ - 1,
                )

        t_unit, t_scale = normal(txt[...].astype(F32))
        w_copy.wait()
        i_unit, i_scale = normal(nn(img[...], w[...]))
        if role == 0:
            kbuf[0, 0, own_rows] = t_unit.astype(BF)
            unit[own_rows] = i_unit
            qf[own_rows] = i_unit.astype(BF)
            raw[own_rows] = img[...]
            away = 4 + 3 + 14 + 16 + at_wrap
            for h in range(2):
                for d in range(8):
                    away = away - jnp.where(is_me(fin_dev(h, d)), 1, 0)
            pl.semaphore_wait(barrier, away)
            text_on(0, 0)
            for u in range(PARTS):
                move(qf.at[pl.ds(u * PART, PART)], kslot(0, 0, 0, u), k_sem(0, 0, 0, u), sibling)
            go(txt, raw.at[own_rows], S_RAW, R_RAW, sibling)
            arrived(raw.at[oth_rows], R_RAW)
            o_unit, oth_scale = normal(nn(raw[oth_rows], w[...]))
        else:
            tbuf[0, 0] = t_unit.astype(BF)
            unit[own_rows] = t_unit
            qf[own_rows] = t_unit.astype(BF)
            kbuf[0, 0, own_rows] = i_unit.astype(BF)
            raw[own_rows] = txt[...]
            pl.semaphore_wait(barrier, 5 + at_wrap + jnp.where(z == 0, 1, 0))
            text_on(0, 0)
            go(img, raw.at[own_rows], S_RAW, R_RAW, sibling)
            image_on(0, 0)
            arrived(raw.at[oth_rows], R_RAW)
            o_unit, oth_scale = normal(raw[oth_rows].astype(F32))
        own_scale = i_scale if role == 0 else t_scale
        unit[oth_rows] = o_unit
        qf[oth_rows] = o_unit.astype(BF)

        gain = jnp.exp(jnp.full((1, 1), nem[0], F32))
        shift = bias[0]

        loss = jnp.zeros((BLOCK, 1), F32)

        def score(t, h, loss):
            k = kbuf[t, h]
            s = gain * nt(qf[...], k) + shift
            e = jnp.exp(-jnp.abs(s))
            sig = jnp.where(s >= 0, 1.0, e) / (1.0 + e)
            label = None
            if t == 0 and h == 0:
                r = lax.broadcasted_iota(jnp.int32, (BLOCK, BLOCK), 0)
                c = lax.broadcasted_iota(jnp.int32, (BLOCK, BLOCK), 1)
                label = jnp.where(r == c, 1.0, 0.0)
                sig = sig - label
            if role == 0:
                term = jnp.maximum(s, 0.0) + jnp.log1p(e)
                if label is not None:
                    term = term - label * s
                loss = loss + jnp.sum(term, axis=1, keepdims=True)
            value = nn((gain * sig).astype(BF), k)
            if label is not None:
                acc[...] = value
            else:
                acc[...] += value
            return loss

        if role == 0:

            def ready(t, h):
                for u in range(PARTS):
                    arrived(kslot(t, h, 1, u), k_sem(t, h, 1, u))

            ready(0, 0)
            loss = score(0, 0, loss)
            sel_copy.wait()
            for part in range(4):
                rows = pl.ds(part * (HALF // 2), HALF // 2)
                emb_t[0, rows] = nt(sel[rows], raw[...]).astype(BF)
            for d in range(1, NX):
                go(emb_t.at[0], emb_t.at[d], S_EMB + d - 1, R_EMB + d - 1, x_dev(d))
            relay_text(0)
            text_on(1, 0)
            relay_text(1)
            text_on(0, 1)
            ready(1, 0)
            loss = score(1, 0, loss)
            text_on(1, 1)
            ready(0, 1)
            loss = score(0, 1, loss)
            text_on(2, 0)
            ready(2, 0)
            loss = score(2, 0, loss)
            ready(1, 1)
            loss = score(1, 1, loss)
            text_on(2, 1)
            ready(2, 1)
            loss = score(2, 1, loss)
        else:
            relay_text(0)
            relay_image(0)
            text_on(1, 0)
            image_on(1, 0)
            relay_text(1)
            text_on(0, 1, range(PARTS // 2))
            for s, u in BOTH:
                move(kslot(0, 0, s, u), kslot(0, 1, s, u), k_sem(0, 1, s, u), across)
            text_on(0, 1, range(PARTS // 2, PARTS))
            relay_image(1)
            loss = score(0, 0, loss)
            text_on(1, 1)
            loss = score(1, 0, loss)
            image_on(0, 1, BOTH[:2])
            for i in range(2 * PARTS - 2):
                image_on(1, 1, BOTH[i : i + 1])
                image_on(0, 1, BOTH[i + 2 : i + 3])
            loss = score(0, 1, loss)
            image_on(1, 1, BOTH[2 * PARTS - 2 :])
            loss = score(1, 1, loss)
            for h in range(2):
                image_on(2, h)
                loss = score(2, h, loss)

        for half_rows, scale in ((own_rows, own_scale), (oth_rows, oth_scale)):
            u = unit[half_rows]
            a = acc[half_rows]
            along = jnp.sum(u * a, axis=1, keepdims=True)
            g = scale * (a - u * along)
            if role == 0:
                pre[half_rows] = g.astype(BF)
                pre_t[:, half_rows] = jnp.transpose(g).astype(BF)
                part = 0 if half_rows is own_rows else 1
                for d in range(1, NX):
                    start = pl.multiple_of(lax.rem(x + d, NX) * COLS, 16)
                    go(
                        pre_t.at[pl.ds(start, COLS), half_rows], p_t.at[d, :, half_rows],
                        S_PRE + 2 * d - 2 + part, R_PRE + 2 * d - 2 + part, x_dev(d),
                    )
            elif half_rows is own_rows:
                tg_o[...] = g
            else:
                unit[half_rows] = g

        if role == 0:
            go(pre.at[oth_rows], sib_bf, S_SIB, R_SIB, sibling)
            turned = jnp.transpose(jnp.broadcast_to(loss, (BLOCK, 128)))
            loss_o[...] = turned[0:1, 0:ROWS]
            loss_s[...] = turned[0:8, ROWS:BLOCK]
            go(loss_s, loss_r, S_LOSS, R_LOSS, sibling)
            start = pl.multiple_of(x * COLS, 16)
            p_t[0] = pre_t[pl.ds(start, COLS)]
            for d in range(1, NX):
                for part in range(2):
                    arrived(p_t.at[d, :, pl.ds(part * ROWS, ROWS)], R_PRE + 2 * d - 2 + part)
                arrived(emb_t.at[d], R_EMB + d - 1)

            def piece(h, d):
                index = lax.rem((y if h == 0 else z) + d, 8)
                return pl.ds(pl.multiple_of(h * HALF + index * PIECE, 16), PIECE)

            totals = []
            for h in range(2):
                for tile in range(2):
                    rows = pl.ds(h * HALF + tile * (HALF // 2), HALF // 2)
                    total = nt(emb_t[0, rows], p_t[0])
                    for k in range(1, NX):
                        total = total + nt(emb_t[k, rows], p_t[k])
                    p_f32[rows] = total
                    p_out[rows] = total.astype(BF)
                for d in (4, 3, 5, 2, 6, 1, 7):
                    i = 7 * h + d - 1
                    go(p_out.at[piece(h, d)], one.at[i], S_ONE + i, R_ONE + i, one_dev(h, d))
            for h in range(2):
                totals.append(p_f32[piece(h, 0)])
            ig_o[...] = nt(pre[own_rows], w[...])
            r = lax.broadcasted_iota(jnp.int32, (128, PIECE), 0)
            c = lax.broadcasted_iota(jnp.int32, (128, PIECE), 1)
            inner = jnp.bitwise_and(r, 15)
            pick = jnp.logical_and(inner < 9, c == 9 * jnp.right_shift(r, 4) + inner)
            pick = jnp.where(pick, 1.0, 0.0).astype(BF)
            for h in range(2):
                total = totals[h]
                for d in range(1, 8):
                    i = 7 * h + d - 1
                    arrived(one.at[i], R_ONE + i)
                    total = total + one[i].astype(F32)
                blocks = nn(pick, total.astype(BF)).astype(BF)
                for i in range(8):
                    fin_s[h, i] = blocks[16 * i : 16 * i + 16]
                for d in range(8):
                    device = fin_dev(h, d)
                    block = fin_block(h, d)
                    me = is_me(device)
                    c = copy(fin_s.at[h, block], fin_r.at[d], S_FIN + 8 * h + d, R_FIN + d, device)

                    @pl.when(me)
                    def _(d=d, block=block, h=h):
                        fin_r[d] = fin_s[h, block]

                    @pl.when(jnp.logical_not(me))
                    def _(c=c):
                        c.start()

            arrived(sib_f32, R_SIB)
            tg_o[...] = sib_f32[...]
        else:
            go(unit.at[oth_rows], sib_f32, S_SIB, R_SIB, sibling)
            arrived(sib_bf, R_SIB)
            ig_o[...] = nt(sib_bf[...], w[...])
            arrived(loss_r, R_LOSS)
            loss_o[...] = loss_r[0:1]

        for d in range(8):
            me = is_me(fin_from(d))

            @pl.when(jnp.logical_not(me))
            def _(d=d):
                arrived(fin_r.at[d], R_FIN + d)

        total = fin_r[0].astype(F32)
        for d in range(1, 8):
            total = total + fin_r[d].astype(F32)
        hg_o[...] = total[0:9]
        for c in started:
            c.wait_send()
        for c, where in later:
            pl.when(z == where)(lambda c=c: c.wait_send())
        if role == 0:
            for h in range(2):
                for d in range(8):
                    device = fin_dev(h, d)
                    c = copy(
                        fin_s.at[h, fin_block(h, d)], fin_r.at[d], S_FIN + 8 * h + d, R_FIN + d, device
                    )
                    pl.when(jnp.logical_not(is_me(device)))(lambda c=c: c.wait_send())

    pl.when(core == 0)(lambda: run(0))
    pl.when(core == 1)(lambda: run(1))


def results(loss, ig, tg, hg, loss_o, ig_o, tg_o, hg_o):
    loss_o[...] = loss[0, :]
    ig_o[...] = ig[...]
    tg_o[...] = tg[...]
    hg_o[...] = hg[...]


def body(image_emb, text_emb, head_weight, natural_exponent_multiplier, bias):
    vmem = pl.BlockSpec(memory_space=pltpu.VMEM)
    smem = pl.BlockSpec(memory_space=pltpu.SMEM)
    hbm = pl.BlockSpec(memory_space=pl.ANY)
    loss, image_grad, text_grad, head_grad = pl.pallas_call(
        kernel,
        name="contrast",
        out_shape=(
            jax.ShapeDtypeStruct((1, ROWS), F32),
            jax.ShapeDtypeStruct((ROWS, D), F32),
            jax.ShapeDtypeStruct((ROWS, D), F32),
            jax.ShapeDtypeStruct((9, COLS), F32),
        ),
        in_specs=[smem, smem, vmem, vmem, hbm, hbm],
        out_specs=(vmem, vmem, vmem, vmem),
        scratch_shapes=[
            pltpu.VMEM((D, D), BF),
            pltpu.VMEM((2 * HALF, D), BF),
            pltpu.VMEM((WINDOW, 2, BLOCK, D), BF),
            pltpu.VMEM((WINDOW, 2, ROWS, D), BF),
            pltpu.VMEM((2, ROWS, D), BF),
            pltpu.VMEM((2, BLOCK, D), BF),
            pltpu.VMEM((BLOCK, D), BF),
            pltpu.VMEM((BLOCK, D), BF),
            pltpu.VMEM((BLOCK, D), F32),
            pltpu.VMEM((BLOCK, D), F32),
            pltpu.VMEM((BLOCK, D), BF),
            pltpu.VMEM((D, BLOCK), BF),
            pltpu.VMEM((ROWS, D), F32),
            pltpu.VMEM((ROWS, D), BF),
            pltpu.VMEM((8, ROWS), F32),
            pltpu.VMEM((8, ROWS), F32),
            pltpu.VMEM((NX, 2 * HALF, BLOCK), BF),
            pltpu.VMEM((NX, COLS, BLOCK), BF),
            pltpu.VMEM((2 * HALF, COLS), BF),
            pltpu.VMEM((2 * HALF, COLS), F32),
            pltpu.VMEM((14, PIECE, COLS), BF),
            pltpu.VMEM((2, 8, 16, COLS), BF),
            pltpu.VMEM((8, 16, COLS), BF),
            pltpu.SemaphoreType.DMA((S_ALL,)),
            pltpu.SemaphoreType.DMA((R_ALL,)),
            pltpu.SemaphoreType.DMA((2,)),
        ],
        compiler_params=pltpu.CompilerParams(
            collective_id=0, has_side_effects=True, vmem_limit_bytes=56 * 2**20
        ),
    )(
        natural_exponent_multiplier,
        bias,
        image_emb,
        text_emb,
        head_weight,
        jnp.asarray(select_matrix(), BF),
    )
    return tuple(
        pl.pallas_call(
            results,
            name="results",
            out_shape=(
                jax.ShapeDtypeStruct((ROWS,), F32),
                jax.ShapeDtypeStruct((ROWS, D), F32),
                jax.ShapeDtypeStruct((ROWS, D), F32),
                jax.ShapeDtypeStruct((9, COLS), F32),
            ),
            in_specs=[vmem] * 4,
            out_specs=(vmem,) * 4,
        )(loss, image_grad, text_grad, head_grad)
    )


def solution(mesh):
    return jax.shard_map(
        body,
        mesh=mesh,
        in_specs=(P(("dp", "pair"), None), P(("dp", "pair"), None), P(), P(), P()),
        out_specs=(
            P(("dp", "pair")),
            P(("dp", "pair"), None),
            P(("dp", "pair"), None),
            P("dp", "pair"),
        ),
        check_vma=False,
    )
```

```python
import jax
import jax.numpy as jnp
import numpy as np
from jax import lax
from jax.experimental import pallas as pl
from jax.experimental.pallas import tpu as pltpu
from jax.sharding import PartitionSpec as P

NX, NYL, NZ = 4, 4, 8
NY = 2 * NYL
WINDOW = 3
ROWS = 128
BLOCK = 2 * ROWS
D = 1152
COLS = D // 4
PIECE = 80
PART = 64
PARTS = ROWS // PART
BOTH = tuple((s, u) for s in (1, 0) for u in range(PARTS))
HALF = 8 * PIECE
EPS = 1e-06
BF = jnp.bfloat16
F32 = jnp.float32

R_RAW, R_SIB, R_LOSS, R_EMB, R_PRE, R_ONE, R_FIN, R_K = 0, 1, 2, 3, 6, 12, 26, 34
R_TEXT = R_K + 12 * PARTS
R_RT = R_TEXT + 6 * PARTS
R_RI = R_RT + 2 * PARTS
R_ALL = R_RI + 4 * PARTS
S_RAW, S_SIB, S_LOSS, S_EMB, S_PRE, S_ONE, S_FIN, S_RT = 0, 1, 2, 3, 6, 12, 26, 42
S_RI = S_RT + 2 * PARTS
S_K = S_RI + 4 * PARTS
S_ALL = S_K + 24 * PARTS


def nt(left, right):
    return lax.dot_general(left, right, (((1,), (1,)), ((), ())), preferred_element_type=F32)


def nn(left, right):
    return jnp.dot(left, right, preferred_element_type=F32)


def select_matrix():
    row = np.arange(2 * HALF)
    half, piece, k = row // HALF, (row % HALF) // PIECE, row % PIECE
    block, inner = k // 9, k % 9
    source = np.where(half == 0, 72 * piece + k, 576 + 72 * block + 9 * piece + inner)
    return ((source[:, None] == np.arange(D)[None, :]) & (k < 72)[:, None]).astype(np.float32)


def kernel(
    nem, bias, img, txt, w_any, sel_any,
    loss_o, ig_o, tg_o, hg_o,
    w, sel, kbuf, tbuf, rt, ri, raw, qf, unit, acc, pre, pre_t, sib_f32, sib_bf, loss_s, loss_r,
    emb_t, p_t, p_out, p_f32, one, fin_s, fin_r, ssem, rsem, lsem,
):
    dp = lax.axis_index("dp")
    pair = lax.axis_index("pair")
    core = lax.rem(pair, 2)
    yh = lax.div(pair, 2)
    x = lax.div(dp, NYL * NZ)
    yl = lax.rem(lax.div(dp, NZ), NYL)
    z = lax.rem(dp, NZ)
    y = yh * NYL + yl

    def chip(cx, cy, cz, cc):
        return (cx * (NYL * NZ) + lax.rem(cy, NYL) * NZ + cz, lax.div(cy, NYL) * 2 + cc)

    sibling = (dp, yh * 2 + 1 - core)
    across = (dp, (1 - yh) * 2 + core)
    flip_to = jnp.where(lax.rem(dp, 32) == 31 * (1 - core), 1, 0)
    flip_from = jnp.where(lax.rem(dp, 32) == 31 * core, 1, 0)
    chain_to = (lax.rem(dp + 1 + 126 * core, 128), lax.rem(yh + flip_to, 2) * 2 + core)
    chain_from = (lax.rem(dp + 127 - 126 * core, 128), lax.rem(yh + flip_from, 2) * 2 + core)

    column = (lax.rem(dp + jnp.where(z == 0, 7, 121), 128), pair)
    row_up = (lax.rem(dp + 8, 128), lax.rem(yh + jnp.where(yl == 3, 1, 0), 2) * 2 + core)
    row_down = (lax.rem(dp + 120, 128), lax.rem(yh + jnp.where(yl == 0, 1, 0), 2) * 2 + core)

    def x_dev(d):
        return chip(lax.rem(x + d, NX), y, z, core)

    def one_dev(h, d):
        if h == 0:
            return chip(x, lax.rem(y + d, NY), z, core)
        return chip(x, y, lax.rem(z + d, NZ), core)

    def fin_block(h, d):
        return lax.rem(z + d, 8) if h == 0 else lax.rem(y + d, 8)

    def fin_dev(h, d):
        block = fin_block(h, d)
        return (8 * y + block if h == 0 else 64 + 8 * block + z, x)

    low = jnp.where(dp < 64, 1, 0)
    q8 = lax.rem(lax.div(dp, 8), 8)

    def fin_from(d):
        ys = jnp.where(low == 1, q8, lax.rem(q8 + 8 - d, 8))
        zs = jnp.where(low == 1, lax.rem(z + 8 - d, 8), z)
        return chip(pair, ys, zs, 0)

    def is_me(device):
        return jnp.logical_and(device[0] == dp, device[1] == pair)

    barrier = pltpu.get_barrier_semaphore()

    def hello(device):
        pl.semaphore_signal(barrier, inc=1, device_id=device, device_id_type=pl.DeviceIdType.MESH)

    def copy(src, dst, send, recv, device):
        return pltpu.make_async_remote_copy(
            src_ref=src, dst_ref=dst, send_sem=ssem.at[send], recv_sem=rsem.at[recv],
            device_id=device, device_id_type=pl.DeviceIdType.MESH,
        )

    def normal(value):
        scale = lax.rsqrt(jnp.sum(value * value, axis=1, keepdims=True) + EPS)
        return value * scale, scale

    def run(role):
        own, oth = role, 1 - role
        own_rows = pl.ds(own * ROWS, ROWS)
        oth_rows = pl.ds(oth * ROWS, ROWS)
        w_copy = pltpu.make_async_copy(w_any, w, lsem.at[0])
        w_copy.start()
        hello(sibling)
        hello(across)
        hello(chain_from)
        hello(chain_to)

        @pl.when(z == 0)
        def _():
            hello(column)
            hello(row_down)

        if role == 1:

            @pl.when(z == NZ - 1)
            def _():
                hello(column)
                hello(row_up)

        if role == 0:
            hello((chain_from[0], chain_from[1] + 1))
            pl.when(z == 0)(lambda: hello((row_down[0], row_down[1] + 1)))

        at_wrap = jnp.where(jnp.logical_or(z == 0, z == NZ - 1), 1 + role, 0)
        if role == 0:
            sel_copy = pltpu.make_async_copy(sel_any, sel, lsem.at[1])
            sel_copy.start()
            for d in range(1, NX):
                hello(x_dev(NX - d))
            for h in range(2):
                for d in range(1, 8):
                    hello(one_dev(h, 8 - d))
        for d in range(8):
            device = fin_from(d)
            pl.when(jnp.logical_not(is_me(device)))(lambda device=device: hello(device))

        started = []
        next_send = [S_K]

        def go(*args):
            c = copy(*args)
            c.start()
            started.append(c)

        def move(src, dst, recv, device):
            go(src, dst, next_send[0], recv, device)
            next_send[0] += 1

        def kslot(t, h, s, u):
            return kbuf.at[t, h, pl.ds(s * ROWS + u * PART, PART)]

        def k_sem(t, h, s, u):
            return R_K + (4 * t + 2 * h + s) * PARTS + u

        def arrived(dst, recv):
            copy(dst, dst, 0, recv, sibling).wait_recv()

        text_to = chain_to if role == 0 else chain_from

        def tslot(t, h, u):
            return kslot(t, h, 0, u) if role == 0 else tbuf.at[t, h, pl.ds(u * PART, PART)]

        def t_sem(t, h, u):
            return R_TEXT + (2 * t + h) * PARTS + u

        def text_next(t, h, u):
            if role == 1 and t == 1:
                return kslot(2, h, 1, u), k_sem(2, h, 1, u), (text_to[0], text_to[1] - 1)
            return tslot(t + 1, h, u), t_sem(t + 1, h, u), text_to

        def chain(src, dst, recv, device, h, wrap, relay_dst, relay_recv):
            if h == 1:
                move(src, dst, recv, device)
                return
            direct = copy(src, dst, next_send[0], recv, device)
            relayed = copy(src, relay_dst, next_send[0], relay_recv, column)
            next_send[0] += 1
            pl.when(z != wrap)(lambda: direct.start())
            pl.when(z == wrap)(lambda: relayed.start())
            started.append(direct)

        def text_on(t, h, parts=range(PARTS)):
            for u in parts:
                if t or h:
                    arrived(tslot(t, h, u), t_sem(t, h, u))
                if t < WINDOW - 1:
                    dst, recv, device = text_next(t, h, u)
                    chain(
                        tslot(t, h, u), dst, recv, device, h,
                        NZ - 1, rt.at[t, pl.ds(u * PART, PART)], R_RT + PARTS * t + u,
                    )
                if t == 0 and h == 0:
                    move(tslot(0, 0, u), tslot(0, 1, u), t_sem(0, 1, u), across)
                if role == 1:
                    move(tslot(t, h, u), kslot(t, h, 1, u), k_sem(t, h, 1, u), sibling)

        def image_on(t, h, parts=BOTH):
            for s, u in parts:
                if t or h or s == 0:
                    arrived(kslot(t, h, s, u), k_sem(t, h, s, u))
                if t < WINDOW - 1:
                    chain(
                        kslot(t, h, s, u), kslot(t + 1, h, s, u), k_sem(t + 1, h, s, u), chain_to, h,
                        0, ri.at[min(t, 1), pl.ds(s * ROWS + u * PART, PART)],
                        R_RI + (2 * t + s) * PARTS + u,
                    )

        later = []

        def relay(src, dst, recv_in, send, recv_out, device, where):
            c = copy(src, dst, send, recv_out, device)

            @pl.when(z == where)
            def _():
                arrived(src, recv_in)
                c.start()

            later.append((c, where))

        def relay_text(t):
            for u in range(PARTS):
                dst, recv, device = text_next(t, 0, u)
                device = (row_up[0], row_up[1] - 1) if device is not text_to else row_up
                relay(
                    rt.at[t, pl.ds(u * PART, PART)], dst, R_RT + PARTS * t + u,
                    S_RT + PARTS * t + u, recv, device, 0,
                )

        def relay_image(t):
            for s, u in BOTH:
                i = (2 * t + s) * PARTS + u
                relay(
                    ri.at[t, pl.ds(s * ROWS + u * PART, PART)], kslot(t + 1, 0, s, u), R_RI + i,
                    S_RI + i, k_sem(t + 1, 0, s, u), row_down, NZ - 1,
                )

        t_unit, t_scale = normal(txt[...].astype(F32))
        w_copy.wait()
        i_unit, i_scale = normal(nn(img[...], w[...]))
        if role == 0:
            kbuf[0, 0, own_rows] = t_unit.astype(BF)
            unit[own_rows] = i_unit
            qf[own_rows] = i_unit.astype(BF)
            raw[own_rows] = img[...]
            away = 4 + 3 + 14 + 16 + at_wrap
            for h in range(2):
                for d in range(8):
                    away = away - jnp.where(is_me(fin_dev(h, d)), 1, 0)
            pl.semaphore_wait(barrier, away)
            text_on(0, 0)
            for u in range(PARTS):
                move(qf.at[pl.ds(u * PART, PART)], kslot(0, 0, 0, u), k_sem(0, 0, 0, u), sibling)
            go(txt, raw.at[own_rows], S_RAW, R_RAW, sibling)
            arrived(raw.at[oth_rows], R_RAW)
            o_unit, oth_scale = normal(nn(raw[oth_rows], w[...]))
        else:
            tbuf[0, 0] = t_unit.astype(BF)
            unit[own_rows] = t_unit
            qf[own_rows] = t_unit.astype(BF)
            kbuf[0, 0, own_rows] = i_unit.astype(BF)
            raw[own_rows] = txt[...]
            pl.semaphore_wait(barrier, 5 + at_wrap + jnp.where(z == 0, 1, 0))
            text_on(0, 0)
            go(img, raw.at[own_rows], S_RAW, R_RAW, sibling)
            image_on(0, 0)
            arrived(raw.at[oth_rows], R_RAW)
            o_unit, oth_scale = normal(raw[oth_rows].astype(F32))
        own_scale = i_scale if role == 0 else t_scale
        unit[oth_rows] = o_unit
        qf[oth_rows] = o_unit.astype(BF)

        gain = jnp.exp(jnp.full((1, 1), nem[0], F32))
        shift = bias[0]

        loss = jnp.zeros((BLOCK, 1), F32)

        def score(t, h, loss):
            k = kbuf[t, h]
            s = gain * nt(qf[...], k) + shift
            e = jnp.exp(-jnp.abs(s))
            sig = jnp.where(s >= 0, 1.0, e) / (1.0 + e)
            label = None
            if t == 0 and h == 0:
                r = lax.broadcasted_iota(jnp.int32, (BLOCK, BLOCK), 0)
                c = lax.broadcasted_iota(jnp.int32, (BLOCK, BLOCK), 1)
                label = jnp.where(r == c, 1.0, 0.0)
                sig = sig - label
            if role == 0:
                term = jnp.maximum(s, 0.0) + jnp.log1p(e)
                if label is not None:
                    term = term - label * s
                loss = loss + jnp.sum(term, axis=1, keepdims=True)
            value = nn((gain * sig).astype(BF), k)
            if label is not None:
                acc[...] = value
            else:
                acc[...] += value
            return loss

        if role == 0:

            def ready(t, h):
                for u in range(PARTS):
                    arrived(kslot(t, h, 1, u), k_sem(t, h, 1, u))

            ready(0, 0)
            loss = score(0, 0, loss)
            sel_copy.wait()
            for part in range(4):
                rows = pl.ds(part * (HALF // 2), HALF // 2)
                emb_t[0, rows] = nt(sel[rows], raw[...]).astype(BF)
            for d in range(1, NX):
                go(emb_t.at[0], emb_t.at[d], S_EMB + d - 1, R_EMB + d - 1, x_dev(d))
            relay_text(0)
            text_on(1, 0)
            relay_text(1)
            text_on(0, 1)
            ready(1, 0)
            loss = score(1, 0, loss)
            text_on(1, 1)
            ready(0, 1)
            loss = score(0, 1, loss)
            text_on(2, 0)
            ready(2, 0)
            loss = score(2, 0, loss)
            ready(1, 1)
            loss = score(1, 1, loss)
            text_on(2, 1)
            ready(2, 1)
            loss = score(2, 1, loss)
        else:
            relay_text(0)
            relay_image(0)
            text_on(1, 0)
            relay_text(1)
            text_on(0, 1, range(PARTS // 2))
            for s, u in BOTH:
                move(kslot(0, 0, s, u), kslot(0, 1, s, u), k_sem(0, 1, s, u), across)
            text_on(0, 1, range(PARTS // 2, PARTS))
            image_on(1, 0)
            relay_image(1)
            loss = score(0, 0, loss)
            text_on(1, 1)
            loss = score(1, 0, loss)
            image_on(0, 1, BOTH[:2])
            for i in range(2 * PARTS - 2):
                image_on(1, 1, BOTH[i : i + 1])
                image_on(0, 1, BOTH[i + 2 : i + 3])
            loss = score(0, 1, loss)
            image_on(1, 1, BOTH[2 * PARTS - 2 :])
            loss = score(1, 1, loss)
            for h in range(2):
                image_on(2, h)
                loss = score(2, h, loss)

        for half_rows, scale in ((own_rows, own_scale), (oth_rows, oth_scale)):
            u = unit[half_rows]
            a = acc[half_rows]
            along = jnp.sum(u * a, axis=1, keepdims=True)
            g = scale * (a - u * along)
            if role == 0:
                pre[half_rows] = g.astype(BF)
                pre_t[:, half_rows] = jnp.transpose(g).astype(BF)
                part = 0 if half_rows is own_rows else 1
                for d in range(1, NX):
                    start = pl.multiple_of(lax.rem(x + d, NX) * COLS, 16)
                    go(
                        pre_t.at[pl.ds(start, COLS), half_rows], p_t.at[d, :, half_rows],
                        S_PRE + 2 * d - 2 + part, R_PRE + 2 * d - 2 + part, x_dev(d),
                    )
            elif half_rows is own_rows:
                tg_o[...] = g
            else:
                unit[half_rows] = g

        if role == 0:
            go(pre.at[oth_rows], sib_bf, S_SIB, R_SIB, sibling)
            turned = jnp.transpose(jnp.broadcast_to(loss, (BLOCK, 128)))
            loss_o[...] = turned[0:1, 0:ROWS]
            loss_s[...] = turned[0:8, ROWS:BLOCK]
            go(loss_s, loss_r, S_LOSS, R_LOSS, sibling)
            start = pl.multiple_of(x * COLS, 16)
            p_t[0] = pre_t[pl.ds(start, COLS)]
            for d in range(1, NX):
                for part in range(2):
                    arrived(p_t.at[d, :, pl.ds(part * ROWS, ROWS)], R_PRE + 2 * d - 2 + part)
                arrived(emb_t.at[d], R_EMB + d - 1)

            def piece(h, d):
                index = lax.rem((y if h == 0 else z) + d, 8)
                return pl.ds(pl.multiple_of(h * HALF + index * PIECE, 16), PIECE)

            totals = []
            for h in range(2):
                for tile in range(2):
                    rows = pl.ds(h * HALF + tile * (HALF // 2), HALF // 2)
                    total = nt(emb_t[0, rows], p_t[0])
                    for k in range(1, NX):
                        total = total + nt(emb_t[k, rows], p_t[k])
                    p_f32[rows] = total
                    p_out[rows] = total.astype(BF)
                for d in (4, 3, 5, 2, 6, 1, 7):
                    i = 7 * h + d - 1
                    go(p_out.at[piece(h, d)], one.at[i], S_ONE + i, R_ONE + i, one_dev(h, d))
            for h in range(2):
                totals.append(p_f32[piece(h, 0)])
            ig_o[...] = nt(pre[own_rows], w[...])
            r = lax.broadcasted_iota(jnp.int32, (128, PIECE), 0)
            c = lax.broadcasted_iota(jnp.int32, (128, PIECE), 1)
            inner = jnp.bitwise_and(r, 15)
            pick = jnp.logical_and(inner < 9, c == 9 * jnp.right_shift(r, 4) + inner)
            pick = jnp.where(pick, 1.0, 0.0).astype(BF)
            for h in range(2):
                total = totals[h]
                for d in range(1, 8):
                    i = 7 * h + d - 1
                    arrived(one.at[i], R_ONE + i)
                    total = total + one[i].astype(F32)
                blocks = nn(pick, total.astype(BF)).astype(BF)
                for i in range(8):
                    fin_s[h, i] = blocks[16 * i : 16 * i + 16]
                for d in range(8):
                    device = fin_dev(h, d)
                    block = fin_block(h, d)
                    me = is_me(device)
                    c = copy(fin_s.at[h, block], fin_r.at[d], S_FIN + 8 * h + d, R_FIN + d, device)

                    @pl.when(me)
                    def _(d=d, block=block, h=h):
                        fin_r[d] = fin_s[h, block]

                    @pl.when(jnp.logical_not(me))
                    def _(c=c):
                        c.start()

            arrived(sib_f32, R_SIB)
            tg_o[...] = sib_f32[...]
        else:
            go(unit.at[oth_rows], sib_f32, S_SIB, R_SIB, sibling)
            arrived(sib_bf, R_SIB)
            ig_o[...] = nt(sib_bf[...], w[...])
            arrived(loss_r, R_LOSS)
            loss_o[...] = loss_r[0:1]

        for d in range(8):
            me = is_me(fin_from(d))

            @pl.when(jnp.logical_not(me))
            def _(d=d):
                arrived(fin_r.at[d], R_FIN + d)

        total = fin_r[0].astype(F32)
        for d in range(1, 8):
            total = total + fin_r[d].astype(F32)
        hg_o[...] = total[0:9]
        for c in started:
            c.wait_send()
        for c, where in later:
            pl.when(z == where)(lambda c=c: c.wait_send())
        if role == 0:
            for h in range(2):
                for d in range(8):
                    device = fin_dev(h, d)
                    c = copy(
                        fin_s.at[h, fin_block(h, d)], fin_r.at[d], S_FIN + 8 * h + d, R_FIN + d, device
                    )
                    pl.when(jnp.logical_not(is_me(device)))(lambda c=c: c.wait_send())

    pl.when(core == 0)(lambda: run(0))
    pl.when(core == 1)(lambda: run(1))


def results(loss, ig, tg, hg, loss_o, ig_o, tg_o, hg_o):
    loss_o[...] = loss[0, :]
    ig_o[...] = ig[...]
    tg_o[...] = tg[...]
    hg_o[...] = hg[...]


def body(image_emb, text_emb, head_weight, natural_exponent_multiplier, bias):
    vmem = pl.BlockSpec(memory_space=pltpu.VMEM)
    smem = pl.BlockSpec(memory_space=pltpu.SMEM)
    hbm = pl.BlockSpec(memory_space=pl.ANY)
    loss, image_grad, text_grad, head_grad = pl.pallas_call(
        kernel,
        name="contrast",
        out_shape=(
            jax.ShapeDtypeStruct((1, ROWS), F32),
            jax.ShapeDtypeStruct((ROWS, D), F32),
            jax.ShapeDtypeStruct((ROWS, D), F32),
            jax.ShapeDtypeStruct((9, COLS), F32),
        ),
        in_specs=[smem, smem, vmem, vmem, hbm, hbm],
        out_specs=(vmem, vmem, vmem, vmem),
        scratch_shapes=[
            pltpu.VMEM((D, D), BF),
            pltpu.VMEM((2 * HALF, D), BF),
            pltpu.VMEM((WINDOW, 2, BLOCK, D), BF),
            pltpu.VMEM((WINDOW, 2, ROWS, D), BF),
            pltpu.VMEM((2, ROWS, D), BF),
            pltpu.VMEM((2, BLOCK, D), BF),
            pltpu.VMEM((BLOCK, D), BF),
            pltpu.VMEM((BLOCK, D), BF),
            pltpu.VMEM((BLOCK, D), F32),
            pltpu.VMEM((BLOCK, D), F32),
            pltpu.VMEM((BLOCK, D), BF),
            pltpu.VMEM((D, BLOCK), BF),
            pltpu.VMEM((ROWS, D), F32),
            pltpu.VMEM((ROWS, D), BF),
            pltpu.VMEM((8, ROWS), F32),
            pltpu.VMEM((8, ROWS), F32),
            pltpu.VMEM((NX, 2 * HALF, BLOCK), BF),
            pltpu.VMEM((NX, COLS, BLOCK), BF),
            pltpu.VMEM((2 * HALF, COLS), BF),
            pltpu.VMEM((2 * HALF, COLS), F32),
            pltpu.VMEM((14, PIECE, COLS), BF),
            pltpu.VMEM((2, 8, 16, COLS), BF),
            pltpu.VMEM((8, 16, COLS), BF),
            pltpu.SemaphoreType.DMA((S_ALL,)),
            pltpu.SemaphoreType.DMA((R_ALL,)),
            pltpu.SemaphoreType.DMA((2,)),
        ],
        compiler_params=pltpu.CompilerParams(
            collective_id=0, has_side_effects=True, vmem_limit_bytes=56 * 2**20
        ),
    )(
        natural_exponent_multiplier,
        bias,
        image_emb,
        text_emb,
        head_weight,
        jnp.asarray(select_matrix(), BF),
    )
    return tuple(
        pl.pallas_call(
            results,
            name="results",
            out_shape=(
                jax.ShapeDtypeStruct((ROWS,), F32),
                jax.ShapeDtypeStruct((ROWS, D), F32),
                jax.ShapeDtypeStruct((ROWS, D), F32),
                jax.ShapeDtypeStruct((9, COLS), F32),
            ),
            in_specs=[vmem] * 4,
            out_specs=(vmem,) * 4,
        )(loss, image_grad, text_grad, head_grad)
    )


def solution(mesh):
    return jax.shard_map(
        body,
        mesh=mesh,
        in_specs=(P(("dp", "pair"), None), P(("dp", "pair"), None), P(), P(), P()),
        out_specs=(
            P(("dp", "pair")),
            P(("dp", "pair"), None),
            P(("dp", "pair"), None),
            P("dp", "pair"),
        ),
        check_vma=False,
    )
```

```python
import jax
import jax.numpy as jnp
import numpy as np
from jax import lax
from jax.experimental import pallas as pl
from jax.experimental.pallas import tpu as pltpu
from jax.sharding import PartitionSpec as P

NX, NYL, NZ = 4, 4, 8
NY = 2 * NYL
WINDOW = 3
ROWS = 128
BLOCK = 2 * ROWS
D = 1152
COLS = D // 4
PIECE = 80
PART = 64
PARTS = ROWS // PART
BOTH = tuple((s, u) for s in (1, 0) for u in range(PARTS))
HALF = 8 * PIECE
EPS = 1e-06
BF = jnp.bfloat16
F32 = jnp.float32

R_RAW, R_SIB, R_LOSS, R_EMB, R_PRE, R_ONE, R_FIN, R_K = 0, 1, 2, 3, 6, 12, 26, 34
R_TEXT = R_K + 12 * PARTS
R_RT = R_TEXT + 6 * PARTS
R_RI = R_RT + 2 * PARTS
R_ALL = R_RI + 4 * PARTS
S_RAW, S_SIB, S_LOSS, S_EMB, S_PRE, S_ONE, S_FIN, S_RT = 0, 1, 2, 3, 6, 12, 26, 42
S_RI = S_RT + 2 * PARTS
S_K = S_RI + 4 * PARTS
S_ALL = S_K + 24 * PARTS


def nt(left, right):
    return lax.dot_general(left, right, (((1,), (1,)), ((), ())), preferred_element_type=F32)


def nn(left, right):
    return jnp.dot(left, right, preferred_element_type=F32)


def select_matrix():
    row = np.arange(2 * HALF)
    half, piece, k = row // HALF, (row % HALF) // PIECE, row % PIECE
    block, inner = k // 9, k % 9
    source = np.where(half == 0, 72 * piece + k, 576 + 72 * block + 9 * piece + inner)
    return ((source[:, None] == np.arange(D)[None, :]) & (k < 72)[:, None]).astype(np.float32)


def kernel(
    nem, bias, img, txt, w_any, sel_any,
    loss_o, ig_o, tg_o, hg_o,
    w, sel, kbuf, tbuf, rt, ri, raw, qf, unit, acc, pre, pre_t, sib_f32, sib_bf, loss_s, loss_r,
    emb_t, p_t, p_out, p_f32, one, fin_s, fin_r, ssem, rsem, lsem,
):
    dp = lax.axis_index("dp")
    pair = lax.axis_index("pair")
    core = lax.rem(pair, 2)
    yh = lax.div(pair, 2)
    x = lax.div(dp, NYL * NZ)
    yl = lax.rem(lax.div(dp, NZ), NYL)
    z = lax.rem(dp, NZ)
    y = yh * NYL + yl

    def chip(cx, cy, cz, cc):
        return (cx * (NYL * NZ) + lax.rem(cy, NYL) * NZ + cz, lax.div(cy, NYL) * 2 + cc)

    sibling = (dp, yh * 2 + 1 - core)
    across = (dp, (1 - yh) * 2 + core)
    flip_to = jnp.where(lax.rem(dp, 32) == 31 * (1 - core), 1, 0)
    flip_from = jnp.where(lax.rem(dp, 32) == 31 * core, 1, 0)
    chain_to = (lax.rem(dp + 1 + 126 * core, 128), lax.rem(yh + flip_to, 2) * 2 + core)
    chain_from = (lax.rem(dp + 127 - 126 * core, 128), lax.rem(yh + flip_from, 2) * 2 + core)

    column = (lax.rem(dp + jnp.where(z == 0, 7, 121), 128), pair)
    row_up = (lax.rem(dp + 8, 128), lax.rem(yh + jnp.where(yl == 3, 1, 0), 2) * 2 + core)
    row_down = (lax.rem(dp + 120, 128), lax.rem(yh + jnp.where(yl == 0, 1, 0), 2) * 2 + core)

    def x_dev(d):
        return chip(lax.rem(x + d, NX), y, z, core)

    def one_dev(h, d):
        if h == 0:
            return chip(x, lax.rem(y + d, NY), z, core)
        return chip(x, y, lax.rem(z + d, NZ), core)

    def fin_block(h, d):
        return lax.rem(z + d, 8) if h == 0 else lax.rem(y + d, 8)

    def fin_dev(h, d):
        block = fin_block(h, d)
        return (8 * y + block if h == 0 else 64 + 8 * block + z, x)

    low = jnp.where(dp < 64, 1, 0)
    q8 = lax.rem(lax.div(dp, 8), 8)

    def fin_from(d):
        ys = jnp.where(low == 1, q8, lax.rem(q8 + 8 - d, 8))
        zs = jnp.where(low == 1, lax.rem(z + 8 - d, 8), z)
        return chip(pair, ys, zs, 0)

    def is_me(device):
        return jnp.logical_and(device[0] == dp, device[1] == pair)

    barrier = pltpu.get_barrier_semaphore()

    def hello(device):
        pl.semaphore_signal(barrier, inc=1, device_id=device, device_id_type=pl.DeviceIdType.MESH)

    def copy(src, dst, send, recv, device):
        return pltpu.make_async_remote_copy(
            src_ref=src, dst_ref=dst, send_sem=ssem.at[send], recv_sem=rsem.at[recv],
            device_id=device, device_id_type=pl.DeviceIdType.MESH,
        )

    def normal(value):
        scale = lax.rsqrt(jnp.sum(value * value, axis=1, keepdims=True) + EPS)
        return value * scale, scale

    def run(role):
        own, oth = role, 1 - role
        own_rows = pl.ds(own * ROWS, ROWS)
        oth_rows = pl.ds(oth * ROWS, ROWS)
        w_copy = pltpu.make_async_copy(w_any, w, lsem.at[0])
        w_copy.start()
        hello(sibling)
        hello(across)
        hello(chain_from)
        hello(chain_to)

        @pl.when(z == 0)
        def _():
            hello(column)
            hello(row_down)

        if role == 1:

            @pl.when(z == NZ - 1)
            def _():
                hello(column)
                hello(row_up)

        if role == 0:
            hello((chain_from[0], chain_from[1] + 1))
            pl.when(z == 0)(lambda: hello((row_down[0], row_down[1] + 1)))

        at_wrap = jnp.where(jnp.logical_or(z == 0, z == NZ - 1), 1 + role, 0)
        if role == 0:
            sel_copy = pltpu.make_async_copy(sel_any, sel, lsem.at[1])
            sel_copy.start()
            for d in range(1, NX):
                hello(x_dev(NX - d))
            for h in range(2):
                for d in range(1, 8):
                    hello(one_dev(h, 8 - d))
        for d in range(8):
            device = fin_from(d)
            pl.when(jnp.logical_not(is_me(device)))(lambda device=device: hello(device))

        started = []
        next_send = [S_K]

        def go(*args):
            c = copy(*args)
            c.start()
            started.append(c)

        def move(src, dst, recv, device):
            go(src, dst, next_send[0], recv, device)
            next_send[0] += 1

        def kslot(t, h, s, u):
            return kbuf.at[t, h, pl.ds(s * ROWS + u * PART, PART)]

        def k_sem(t, h, s, u):
            return R_K + (4 * t + 2 * h + s) * PARTS + u

        def arrived(dst, recv):
            copy(dst, dst, 0, recv, sibling).wait_recv()

        text_to = chain_to if role == 0 else chain_from

        def tslot(t, h, u):
            return kslot(t, h, 0, u) if role == 0 else tbuf.at[t, h, pl.ds(u * PART, PART)]

        def t_sem(t, h, u):
            return R_TEXT + (2 * t + h) * PARTS + u

        def text_next(t, h, u):
            if role == 1 and t == 1:
                return kslot(2, h, 1, u), k_sem(2, h, 1, u), (text_to[0], text_to[1] - 1)
            return tslot(t + 1, h, u), t_sem(t + 1, h, u), text_to

        def chain(src, dst, recv, device, h, wrap, relay_dst, relay_recv):
            if h == 1:
                move(src, dst, recv, device)
                return
            direct = copy(src, dst, next_send[0], recv, device)
            relayed = copy(src, relay_dst, next_send[0], relay_recv, column)
            next_send[0] += 1
            pl.when(z != wrap)(lambda: direct.start())
            pl.when(z == wrap)(lambda: relayed.start())
            started.append(direct)

        def text_on(t, h, parts=range(PARTS)):
            for u in parts:
                if t or h:
                    arrived(tslot(t, h, u), t_sem(t, h, u))
                if t < WINDOW - 1:
                    dst, recv, device = text_next(t, h, u)
                    chain(
                        tslot(t, h, u), dst, recv, device, h,
                        NZ - 1, rt.at[t, pl.ds(u * PART, PART)], R_RT + PARTS * t + u,
                    )
                if t == 0 and h == 0:
                    move(tslot(0, 0, u), tslot(0, 1, u), t_sem(0, 1, u), across)
                if role == 1:
                    move(tslot(t, h, u), kslot(t, h, 1, u), k_sem(t, h, 1, u), sibling)

        def image_on(t, h, parts=BOTH):
            for s, u in parts:
                if t or h or s == 0:
                    arrived(kslot(t, h, s, u), k_sem(t, h, s, u))
                if t < WINDOW - 1:
                    chain(
                        kslot(t, h, s, u), kslot(t + 1, h, s, u), k_sem(t + 1, h, s, u), chain_to, h,
                        0, ri.at[min(t, 1), pl.ds(s * ROWS + u * PART, PART)],
                        R_RI + (2 * t + s) * PARTS + u,
                    )

        later = []

        def relay(src, dst, recv_in, send, recv_out, device, where):
            c = copy(src, dst, send, recv_out, device)

            @pl.when(z == where)
            def _():
                arrived(src, recv_in)
                c.start()

            later.append((c, where))

        def relay_text(t):
            for u in range(PARTS):
                dst, recv, device = text_next(t, 0, u)
                device = (row_up[0], row_up[1] - 1) if device is not text_to else row_up
                relay(
                    rt.at[t, pl.ds(u * PART, PART)], dst, R_RT + PARTS * t + u,
                    S_RT + PARTS * t + u, recv, device, 0,
                )

        def relay_image(t):
            for s, u in BOTH:
                i = (2 * t + s) * PARTS + u
                relay(
                    ri.at[t, pl.ds(s * ROWS + u * PART, PART)], kslot(t + 1, 0, s, u), R_RI + i,
                    S_RI + i, k_sem(t + 1, 0, s, u), row_down, NZ - 1,
                )

        t_unit, t_scale = normal(txt[...].astype(F32))
        w_copy.wait()
        i_unit, i_scale = normal(nn(img[...], w[...]))
        if role == 0:
            kbuf[0, 0, own_rows] = t_unit.astype(BF)
            unit[own_rows] = i_unit
            qf[own_rows] = i_unit.astype(BF)
            raw[own_rows] = img[...]
            away = 4 + 3 + 14 + 16 + at_wrap
            for h in range(2):
                for d in range(8):
                    away = away - jnp.where(is_me(fin_dev(h, d)), 1, 0)
            pl.semaphore_wait(barrier, away)
            text_on(0, 0)
            for u in range(PARTS):
                move(qf.at[pl.ds(u * PART, PART)], kslot(0, 0, 0, u), k_sem(0, 0, 0, u), sibling)
            go(txt, raw.at[own_rows], S_RAW, R_RAW, sibling)
            arrived(raw.at[oth_rows], R_RAW)
            o_unit, oth_scale = normal(nn(raw[oth_rows], w[...]))
        else:
            tbuf[0, 0] = t_unit.astype(BF)
            unit[own_rows] = t_unit
            qf[own_rows] = t_unit.astype(BF)
            kbuf[0, 0, own_rows] = i_unit.astype(BF)
            raw[own_rows] = txt[...]
            pl.semaphore_wait(barrier, 5 + at_wrap + jnp.where(z == 0, 1, 0))
            text_on(0, 0)
            go(img, raw.at[own_rows], S_RAW, R_RAW, sibling)
            image_on(0, 0)
            arrived(raw.at[oth_rows], R_RAW)
            o_unit, oth_scale = normal(raw[oth_rows].astype(F32))
        own_scale = i_scale if role == 0 else t_scale
        unit[oth_rows] = o_unit
        qf[oth_rows] = o_unit.astype(BF)

        gain = jnp.exp(jnp.full((1, 1), nem[0], F32))
        shift = bias[0]

        loss = jnp.zeros((BLOCK, 1), F32)

        def score(t, h, loss):
            k = kbuf[t, h]
            s = gain * nt(qf[...], k) + shift
            e = jnp.exp(-jnp.abs(s))
            sig = jnp.where(s >= 0, 1.0, e) / (1.0 + e)
            label = None
            if t == 0 and h == 0:
                r = lax.broadcasted_iota(jnp.int32, (BLOCK, BLOCK), 0)
                c = lax.broadcasted_iota(jnp.int32, (BLOCK, BLOCK), 1)
                label = jnp.where(r == c, 1.0, 0.0)
                sig = sig - label
            if role == 0:
                term = jnp.maximum(s, 0.0) + jnp.log1p(e)
                if label is not None:
                    term = term - label * s
                loss = loss + jnp.sum(term, axis=1, keepdims=True)
            value = nn((gain * sig).astype(BF), k)
            if label is not None:
                acc[...] = value
            else:
                acc[...] += value
            return loss

        if role == 0:

            def ready(t, h):
                for u in range(PARTS):
                    arrived(kslot(t, h, 1, u), k_sem(t, h, 1, u))

            ready(0, 0)
            loss = score(0, 0, loss)
            sel_copy.wait()
            for part in range(4):
                rows = pl.ds(part * (HALF // 2), HALF // 2)
                emb_t[0, rows] = nt(sel[rows], raw[...]).astype(BF)
            for d in range(1, NX):
                go(emb_t.at[0], emb_t.at[d], S_EMB + d - 1, R_EMB + d - 1, x_dev(d))
            relay_text(0)
            text_on(1, 0)
            relay_text(1)
            text_on(0, 1)
            ready(1, 0)
            loss = score(1, 0, loss)
            text_on(1, 1)
            ready(0, 1)
            loss = score(0, 1, loss)
            text_on(2, 0)
            ready(2, 0)
            loss = score(2, 0, loss)
            ready(1, 1)
            loss = score(1, 1, loss)
            text_on(2, 1)
            ready(2, 1)
            loss = score(2, 1, loss)
        else:
            relay_text(0)
            relay_image(0)
            text_on(1, 0)
            relay_text(1)
            text_on(0, 1, range(PARTS // 2))
            for s, u in BOTH:
                move(kslot(0, 0, s, u), kslot(0, 1, s, u), k_sem(0, 1, s, u), across)
            text_on(0, 1, range(PARTS // 2, PARTS))
            image_on(1, 0)
            relay_image(1)
            text_on(1, 1)
            loss = score(0, 0, loss)
            image_on(0, 1, BOTH[:2])
            for i in range(2 * PARTS - 2):
                image_on(1, 1, BOTH[i : i + 1])
                image_on(0, 1, BOTH[i + 2 : i + 3])
            loss = score(1, 0, loss)
            loss = score(0, 1, loss)
            image_on(1, 1, BOTH[2 * PARTS - 2 :])
            loss = score(1, 1, loss)
            for h in range(2):
                image_on(2, h)
                loss = score(2, h, loss)

        for half_rows, scale in ((own_rows, own_scale), (oth_rows, oth_scale)):
            u = unit[half_rows]
            a = acc[half_rows]
            along = jnp.sum(u * a, axis=1, keepdims=True)
            g = scale * (a - u * along)
            if role == 0:
                pre[half_rows] = g.astype(BF)
                pre_t[:, half_rows] = jnp.transpose(g).astype(BF)
                part = 0 if half_rows is own_rows else 1
                for d in range(1, NX):
                    start = pl.multiple_of(lax.rem(x + d, NX) * COLS, 16)
                    go(
                        pre_t.at[pl.ds(start, COLS), half_rows], p_t.at[d, :, half_rows],
                        S_PRE + 2 * d - 2 + part, R_PRE + 2 * d - 2 + part, x_dev(d),
                    )
            elif half_rows is own_rows:
                tg_o[...] = g
            else:
                unit[half_rows] = g

        if role == 0:
            go(pre.at[oth_rows], sib_bf, S_SIB, R_SIB, sibling)
            turned = jnp.transpose(jnp.broadcast_to(loss, (BLOCK, 128)))
            loss_o[...] = turned[0:1, 0:ROWS]
            loss_s[...] = turned[0:8, ROWS:BLOCK]
            go(loss_s, loss_r, S_LOSS, R_LOSS, sibling)
            start = pl.multiple_of(x * COLS, 16)
            p_t[0] = pre_t[pl.ds(start, COLS)]
            for d in range(1, NX):
                for part in range(2):
                    arrived(p_t.at[d, :, pl.ds(part * ROWS, ROWS)], R_PRE + 2 * d - 2 + part)
                arrived(emb_t.at[d], R_EMB + d - 1)

            def piece(h, d):
                index = lax.rem((y if h == 0 else z) + d, 8)
                return pl.ds(pl.multiple_of(h * HALF + index * PIECE, 16), PIECE)

            totals = []
            for h in range(2):
                for tile in range(2):
                    rows = pl.ds(h * HALF + tile * (HALF // 2), HALF // 2)
                    total = nt(emb_t[0, rows], p_t[0])
                    for k in range(1, NX):
                        total = total + nt(emb_t[k, rows], p_t[k])
                    p_f32[rows] = total
                    p_out[rows] = total.astype(BF)
                for d in (4, 3, 5, 2, 6, 1, 7):
                    i = 7 * h + d - 1
                    go(p_out.at[piece(h, d)], one.at[i], S_ONE + i, R_ONE + i, one_dev(h, d))
            for h in range(2):
                totals.append(p_f32[piece(h, 0)])
            ig_o[...] = nt(pre[own_rows], w[...])
            r = lax.broadcasted_iota(jnp.int32, (128, PIECE), 0)
            c = lax.broadcasted_iota(jnp.int32, (128, PIECE), 1)
            inner = jnp.bitwise_and(r, 15)
            pick = jnp.logical_and(inner < 9, c == 9 * jnp.right_shift(r, 4) + inner)
            pick = jnp.where(pick, 1.0, 0.0).astype(BF)
            for h in range(2):
                total = totals[h]
                for d in range(1, 8):
                    i = 7 * h + d - 1
                    arrived(one.at[i], R_ONE + i)
                    total = total + one[i].astype(F32)
                blocks = nn(pick, total.astype(BF)).astype(BF)
                for i in range(8):
                    fin_s[h, i] = blocks[16 * i : 16 * i + 16]
                for d in range(8):
                    device = fin_dev(h, d)
                    block = fin_block(h, d)
                    me = is_me(device)
                    c = copy(fin_s.at[h, block], fin_r.at[d], S_FIN + 8 * h + d, R_FIN + d, device)

                    @pl.when(me)
                    def _(d=d, block=block, h=h):
                        fin_r[d] = fin_s[h, block]

                    @pl.when(jnp.logical_not(me))
                    def _(c=c):
                        c.start()

            arrived(sib_f32, R_SIB)
            tg_o[...] = sib_f32[...]
        else:
            go(unit.at[oth_rows], sib_f32, S_SIB, R_SIB, sibling)
            arrived(sib_bf, R_SIB)
            ig_o[...] = nt(sib_bf[...], w[...])
            arrived(loss_r, R_LOSS)
            loss_o[...] = loss_r[0:1]

        for d in range(8):
            me = is_me(fin_from(d))

            @pl.when(jnp.logical_not(me))
            def _(d=d):
                arrived(fin_r.at[d], R_FIN + d)

        total = fin_r[0].astype(F32)
        for d in range(1, 8):
            total = total + fin_r[d].astype(F32)
        hg_o[...] = total[0:9]
        for c in started:
            c.wait_send()
        for c, where in later:
            pl.when(z == where)(lambda c=c: c.wait_send())
        if role == 0:
            for h in range(2):
                for d in range(8):
                    device = fin_dev(h, d)
                    c = copy(
                        fin_s.at[h, fin_block(h, d)], fin_r.at[d], S_FIN + 8 * h + d, R_FIN + d, device
                    )
                    pl.when(jnp.logical_not(is_me(device)))(lambda c=c: c.wait_send())

    pl.when(core == 0)(lambda: run(0))
    pl.when(core == 1)(lambda: run(1))


def results(loss, ig, tg, hg, loss_o, ig_o, tg_o, hg_o):
    loss_o[...] = loss[0, :]
    ig_o[...] = ig[...]
    tg_o[...] = tg[...]
    hg_o[...] = hg[...]


def body(image_emb, text_emb, head_weight, natural_exponent_multiplier, bias):
    vmem = pl.BlockSpec(memory_space=pltpu.VMEM)
    smem = pl.BlockSpec(memory_space=pltpu.SMEM)
    hbm = pl.BlockSpec(memory_space=pl.ANY)
    loss, image_grad, text_grad, head_grad = pl.pallas_call(
        kernel,
        name="contrast",
        out_shape=(
            jax.ShapeDtypeStruct((1, ROWS), F32),
            jax.ShapeDtypeStruct((ROWS, D), F32),
            jax.ShapeDtypeStruct((ROWS, D), F32),
            jax.ShapeDtypeStruct((9, COLS), F32),
        ),
        in_specs=[smem, smem, vmem, vmem, hbm, hbm],
        out_specs=(vmem, vmem, vmem, vmem),
        scratch_shapes=[
            pltpu.VMEM((D, D), BF),
            pltpu.VMEM((2 * HALF, D), BF),
            pltpu.VMEM((WINDOW, 2, BLOCK, D), BF),
            pltpu.VMEM((WINDOW, 2, ROWS, D), BF),
            pltpu.VMEM((2, ROWS, D), BF),
            pltpu.VMEM((2, BLOCK, D), BF),
            pltpu.VMEM((BLOCK, D), BF),
            pltpu.VMEM((BLOCK, D), BF),
            pltpu.VMEM((BLOCK, D), F32),
            pltpu.VMEM((BLOCK, D), F32),
            pltpu.VMEM((BLOCK, D), BF),
            pltpu.VMEM((D, BLOCK), BF),
            pltpu.VMEM((ROWS, D), F32),
            pltpu.VMEM((ROWS, D), BF),
            pltpu.VMEM((8, ROWS), F32),
            pltpu.VMEM((8, ROWS), F32),
            pltpu.VMEM((NX, 2 * HALF, BLOCK), BF),
            pltpu.VMEM((NX, COLS, BLOCK), BF),
            pltpu.VMEM((2 * HALF, COLS), BF),
            pltpu.VMEM((2 * HALF, COLS), F32),
            pltpu.VMEM((14, PIECE, COLS), BF),
            pltpu.VMEM((2, 8, 16, COLS), BF),
            pltpu.VMEM((8, 16, COLS), BF),
            pltpu.SemaphoreType.DMA((S_ALL,)),
            pltpu.SemaphoreType.DMA((R_ALL,)),
            pltpu.SemaphoreType.DMA((2,)),
        ],
        compiler_params=pltpu.CompilerParams(
            collective_id=0, has_side_effects=True, vmem_limit_bytes=56 * 2**20
        ),
    )(
        natural_exponent_multiplier,
        bias,
        image_emb,
        text_emb,
        head_weight,
        jnp.asarray(select_matrix(), BF),
    )
    return tuple(
        pl.pallas_call(
            results,
            name="results",
            out_shape=(
                jax.ShapeDtypeStruct((ROWS,), F32),
                jax.ShapeDtypeStruct((ROWS, D), F32),
                jax.ShapeDtypeStruct((ROWS, D), F32),
                jax.ShapeDtypeStruct((9, COLS), F32),
            ),
            in_specs=[vmem] * 4,
            out_specs=(vmem,) * 4,
        )(loss, image_grad, text_grad, head_grad)
    )


def solution(mesh):
    return jax.shard_map(
        body,
        mesh=mesh,
        in_specs=(P(("dp", "pair"), None), P(("dp", "pair"), None), P(), P(), P()),
        out_specs=(
            P(("dp", "pair")),
            P(("dp", "pair"), None),
            P(("dp", "pair"), None),
            P("dp", "pair"),
        ),
        check_vma=False,
    )
```
